32 devices in a mesh: ctx: 32 (over z, y, x, core), seq: 1.
Axes of the slice: x: 2, y: 2, z: 4, core: 2. Of those that a mesh axis runs over, the one named last changes fastest.
Arguments:
- query_states: bfloat16 [4096, 4096], P(('seq', 'ctx')), may hold values from -6.5 to 6.5
- key_states: bfloat16 [4096, 512], P(('seq', 'ctx')), may hold values from -4 to 4
- value_states: bfloat16 [4096, 512], P(('seq', 'ctx')), may hold values from -4 to 4
- block_docs: int32 [32], P('seq'), may hold values from 0 to 3, never falling along the last dimension, each value on 1 to 12 neighbouring positions
Outputs:
- attended: bfloat16 [4096, 4096], P(('seq', 'ctx'))
The draws below stay inside these ranges and needn't reach their ends.
Inputs may be any that keep to these rules, and one draw needn't show every extreme that they name: block_docs never falls along the sequence; every document covers 1 to min(12, 16) whole blocks, and some document covers exactly that many.
All inputs are finite; a program needn't handle non-finite values.
Results may differ from the reference program's by a relative error of at most 0.004.
Values may be sent and summed in bfloat16 or wider, within the bound.
No kernel may reach another device: no remote copies, remote signals or barrier semaphores. Data moves between devices by JAX's collectives and lax.ppermute only.
A program may use at most 64 MiB of HBM per device.

```python
import math
import jax
import jax.numpy as jnp
import numpy as np
from jax import lax

HQ = 32
KVH = 4
HD = 128
BLK = 128
WIN = 3
TOK_DEV = 128
TOKENS = 4096
NB = 32
N_CTX = 32


def draw_query_states(key, part):
    base = jnp.clip(jax.random.normal(jax.random.fold_in(key, 1), (TOKENS, HQ, HD), jnp.float32), -4.0, 4.0)
    return base.reshape(TOKENS, HQ * HD).astype(jnp.bfloat16)


def draw_key_states(key, part):
    base = jnp.clip(jax.random.normal(jax.random.fold_in(key, 2), (TOKENS, KVH, HD), jnp.float32), -4.0, 4.0)
    return base.reshape(TOKENS, KVH * HD).astype(jnp.bfloat16)


def shard_levels(rng, shape, cuts, low, largest):
    factor_of = 1.0
    for axis_at, blocks in cuts:
        heights = jax.random.uniform(jax.random.fold_in(jax.random.fold_in(rng, 6), axis_at), (blocks,), jnp.float32, low / len(cuts), largest / len(cuts))
        factor_of = factor_of * jnp.repeat(jnp.exp(heights), shape[axis_at] // blocks).reshape((-1,) + (1,) * (len(shape) - 1 - axis_at))
    return factor_of


def split_up(amount, total, limit, lean):
    weights = [(1 << 20) // math.isqrt(grade ** lean) + 1 for grade in range(2, amount + 1)]
    rest, counts = total - limit - (amount - 1), [1] * (amount - 1)
    while rest > 0:
        movable = [i for i in range(amount - 1) if counts[i] < limit]
        whole, remaining = sum([weights[i] for i in movable]), rest
        for i in movable:
            extra = min(limit - counts[i], max(1, remaining * weights[i] // whole), rest)
            counts[i] = counts[i] + extra
            rest = rest - extra
    return np.array([limit] + counts)


def ragged_sizes(stream_key, amount, total, limit, lean):
    if amount == 2:
        one = jax.random.randint(stream_key, (), max(1, total - limit), min(limit, total - 1) + 1)
        return jnp.stack([one, total - one])
    tallies = jnp.asarray(split_up(amount, total, limit, lean), jnp.int32)
    pairs = (amount - 1) // 2
    giver, taker = tallies[1:1 + 2 * pairs:2], tallies[2:2 + 2 * pairs:2]
    room = jnp.minimum(giver - 1, limit - taker)
    passed = jax.random.randint(jax.random.fold_in(stream_key, 1), (pairs,), 0, 1 << 20) % (room + 1)
    tallies = tallies.at[1:1 + 2 * pairs:2].set(giver - passed).at[2:2 + 2 * pairs:2].set(taker + passed)
    return tallies[jax.random.permutation(jax.random.fold_in(stream_key, 2), amount)]


def centred(key, shape, width, bound, pieces=(), kind=jnp.bfloat16):
    entries = width * jax.random.normal(key, shape, jnp.float32)
    if pieces:
        entries = entries * shard_levels(key, shape, pieces, -0.22, 0.18)
    return jnp.clip(entries, -bound, bound).astype(kind)


def setup_inputs(seed: int = 0, part: int = 0) -> dict:
    arg_keys = jax.random.split(jax.random.key(seed), 5)
    part_splits = jax.random.split(jax.random.fold_in(arg_keys[4], part), 5)
    query_states = draw_query_states(jax.random.fold_in(jax.random.fold_in(arg_keys[4], part), 71), part)
    key_states = draw_key_states(jax.random.fold_in(jax.random.fold_in(arg_keys[4], part), 71), part)
    value_states = centred(part_splits[2], (TOKENS, KVH * HD), 1.0, 4.0, ((0, 32),))
    block_docs = jnp.searchsorted(jnp.cumsum(ragged_sizes(part_splits[3], max(NB // 8, 2), NB, min(12 * TOK_DEV // BLK, NB // 2), 2)), jnp.arange(NB), side="right").astype(jnp.int32)
    return dict(query_states=query_states, key_states=key_states, value_states=value_states, block_docs=block_docs)


def reference(query_states, key_states, value_states, block_docs):
    group_size = HQ // KVH
    window_rows = (WIN + 1) * TOK_DEV
    pad_rows = WIN * TOK_DEV
    score_scale = 1.0 / math.sqrt(HD)
    keys_padded = jnp.concatenate([jnp.zeros((pad_rows, KVH * HD), key_states.dtype), key_states], 0)
    values_padded = jnp.concatenate([jnp.zeros((pad_rows, KVH * HD), value_states.dtype), value_states], 0)

    def one_shard(shard_index):
        first_row = (shard_index * TOK_DEV).astype(jnp.int32)
        queries = lax.dynamic_slice_in_dim(query_states, first_row, TOK_DEV, 0).astype(jnp.float32)
        queries = queries.reshape(TOK_DEV, KVH, group_size, HD)
        key_rows = lax.dynamic_slice_in_dim(keys_padded, first_row, window_rows, 0).astype(jnp.float32)
        key_rows = key_rows.reshape(window_rows, KVH, HD)
        value_rows = lax.dynamic_slice_in_dim(values_padded, first_row, window_rows, 0).astype(jnp.float32)
        value_rows = value_rows.reshape(window_rows, KVH, HD)
        scores = jnp.einsum('tkgd,skd->kgts', queries, key_rows) * score_scale
        query_pos = first_row + jnp.arange(TOK_DEV, dtype=jnp.int32)
        key_pos = first_row - pad_rows + jnp.arange(window_rows, dtype=jnp.int32)
        query_doc = block_docs[query_pos // BLK]
        key_doc = block_docs[jnp.maximum(key_pos, 0) // BLK]
        allowed = (key_pos[None, :] >= 0) & (key_pos[None, :] <= query_pos[:, None]) & (query_doc[:, None] == key_doc[None, :])
        masked = jnp.where(allowed, scores, -1e+30)
        row_max = lax.optimization_barrier(jnp.max(masked, axis=-1, keepdims=True))
        exp_weights = jnp.where(allowed, jnp.exp(masked - row_max), 0.0)
        weight_total = lax.optimization_barrier(jnp.sum(exp_weights, axis=-1, keepdims=True))
        rounded = lax.optimization_barrier(exp_weights.astype(jnp.bfloat16))
        weights = rounded.astype(jnp.float32)
        result = jnp.einsum('kgts,skd->kgtd', weights, value_rows) / weight_total
        return result.transpose(2, 0, 1, 3).reshape(TOK_DEV, HQ * HD).astype(jnp.bfloat16)
    shards = lax.map(one_shard, jnp.arange(N_CTX, dtype=jnp.int32))
    return shards.reshape(TOKENS, HQ * HD)
```

```python
import functools
import math

import jax
import jax.numpy as jnp
from jax import lax
from jax.experimental import pallas as pl
from jax.experimental.pallas import tpu as pltpu
from jax.sharding import PartitionSpec as P

HD = 128
BLK = 128
NEG = -1e30
LIMIT = 1e37
EXP2_SCALE = math.log2(math.e) / math.sqrt(HD)
F32 = jnp.float32
BF16 = jnp.bfloat16


def dot_nt(a, b):
    return lax.dot_general(a, b, (((1,), (1,)), ((), ())), preferred_element_type=F32)


def dot_nn(a, b):
    return lax.dot_general(a, b, (((1,), (0,)), ((), ())), preferred_element_type=F32)


def head(ref, index):
    return ref[:, index * HD : (index + 1) * HD]


def group_queries(q_ref, group, size):
    return jnp.concatenate([head(q_ref, group * size + h) for h in range(size)], axis=0)


def with_ones(values):
    return jnp.concatenate([values, jnp.ones_like(values)], axis=1)


def causal_bias(size):
    row = lax.broadcasted_iota(jnp.int32, (BLK, BLK), 0)
    col = lax.broadcasted_iota(jnp.int32, (BLK, BLK), 1)
    bias = jnp.where(col <= row, 0.0, NEG).astype(F32)
    return jnp.concatenate([bias] * size, axis=0)


def visible(docs_ref, position, distance):
    source = position - distance
    same = docs_ref[jnp.maximum(source, 0)] == docs_ref[position]
    return jnp.where((source >= 0) & same, 1, 0)


def masked_keys(keys, seen):
    lane = lax.broadcasted_iota(jnp.int32, keys.shape, 1)
    seen_at = jnp.full(keys.shape, seen, jnp.int32) > 0
    kept = jnp.where(seen_at, keys.astype(F32), 0.0)
    extra = jnp.where(seen_at, jnp.where(lane == 0, 1.0, 0.0), jnp.where(lane == 1, NEG, 0.0))
    return jnp.concatenate([kept, extra], axis=1).astype(BF16)


def own_kernel(groups, size, q_ref, k_ref, v_ref, acc_ref, shift_ref):
    rows = size * BLK
    bias = causal_bias(size)
    lane = lax.broadcasted_iota(jnp.int32, (rows, HD), 1)
    for g in range(groups):
        scores = dot_nt(group_queries(q_ref, g, size), head(k_ref, g)) + bias
        top = jnp.max(scores, axis=1, keepdims=True).astype(BF16).astype(F32)
        weights = jnp.exp2((scores - top) * EXP2_SCALE).astype(BF16)
        acc_ref[g] = dot_nn(weights, with_ones(head(v_ref, g)))
        shift_ref[g] = jnp.where(lane == 0, -top, jnp.where(lane == 1, 1.0, 0.0)).astype(BF16)


def add_kernel(groups, size, docs_ref, pos_ref, q_ref, shift_ref, k_ref, v_ref, acc_ref, out_ref):
    seen = visible(docs_ref, pos_ref[0], 2)
    for g in range(groups):
        queries = jnp.concatenate([group_queries(q_ref, g, size), shift_ref[g]], axis=1)
        scores = dot_nt(queries, masked_keys(head(k_ref, g), seen))
        weights = jnp.exp2(scores * EXP2_SCALE).astype(BF16)
        out_ref[g] = acc_ref[g] + dot_nn(weights, with_ones(head(v_ref, g)))


def last_kernel(
    groups, size, docs_ref, pos_ref, q_ref, shift_ref, acc_ref, kb_ref, vb_ref, kc_ref, vc_ref,
    k0_hbm, v0_hbm, ka_hbm, va_hbm, out_ref, held, sems,
):
    position = pos_ref[0]
    odd = lax.rem(position, 2)
    seen_b = visible(docs_ref, position, 1 + 2 * odd)
    seen_c = visible(docs_ref, position, 3 - 2 * odd)
    worst = jnp.zeros((BLK, HD), F32)
    for g in range(groups):
        queries = jnp.concatenate([group_queries(q_ref, g, size), shift_ref[g]], axis=1)
        keys = [masked_keys(head(kb_ref, g), seen_b), masked_keys(head(kc_ref, g), seen_c)]
        scores = dot_nt(queries, jnp.concatenate(keys, axis=0))
        weights = jnp.exp2(scores * EXP2_SCALE).astype(BF16)
        values = jnp.concatenate([head(vb_ref, g), head(vc_ref, g)], axis=0)
        total = acc_ref[g] + dot_nn(weights, with_ones(values))
        for h in range(size):
            part = total[h * BLK : (h + 1) * BLK]
            worst = jnp.maximum(worst, part[:, HD:])
            at = (g * size + h) * HD
            out_ref[:, at : at + HD] = (part[:, :HD] / part[:, HD:]).astype(BF16)

    @pl.when(jnp.logical_not(jnp.max(worst) < LIMIT))
    def _():
        copies = [
            pltpu.make_async_copy(src, held.at[i], sems.at[i])
            for i, src in enumerate((k0_hbm, v0_hbm, ka_hbm, va_hbm))
        ]
        for copy in copies:
            copy.start()
        for copy in copies:
            copy.wait()
        seen_a = visible(docs_ref, position, 2)
        flags = [jnp.where(s > 0, 0.0, NEG).astype(F32) for s in (seen_a, seen_b, seen_c)]
        row = lax.broadcasted_iota(jnp.int32, (BLK, BLK), 0)
        col = lax.broadcasted_iota(jnp.int32, (BLK, BLK), 1)
        for g in range(groups):

            def one_head(h, _):
                at = pl.ds(pl.multiple_of((g * size + h) * HD, HD), HD)
                queries = q_ref[:, at]
                span = slice(g * HD, (g + 1) * HD)
                keys = (held[0, :, span], held[2, :, span], head(kb_ref, g), head(kc_ref, g))
                values = (held[1, :, span], held[3, :, span], head(vb_ref, g), head(vc_ref, g))
                scores = [dot_nt(queries, k) for k in keys]
                masked = [jnp.where(col <= row, scores[0], NEG)]
                masked += [
                    jnp.where(jnp.full((BLK, BLK), f, F32) < 0, NEG, s)
                    for s, f in zip(scores[1:], flags)
                ]
                tops = [jnp.max(s, axis=1, keepdims=True) for s in masked]
                top = functools.reduce(jnp.maximum, tops)
                weights = [jnp.exp2((s - top) * EXP2_SCALE) for s in masked]
                total = sum(jnp.sum(w, axis=1, keepdims=True) for w in weights)
                product = sum(dot_nn(w.astype(BF16), v) for w, v in zip(weights, values))
                out_ref[:, at] = (product / total).astype(BF16)
                return 0

            lax.fori_loop(0, size, one_head, 0)


VMEM = pl.BlockSpec(memory_space=pltpu.VMEM)
SMEM = pl.BlockSpec(memory_space=pltpu.SMEM)
ANY = pl.BlockSpec(memory_space=pl.ANY)
PARAMS = pltpu.CompilerParams(vmem_limit_bytes=40 * 1024 * 1024)


def on_device(queries, keys, values, docs):
    row_count = queries.shape[0]
    groups = keys.shape[1] // HD
    size = queries.shape[1] // keys.shape[1]
    rows = size * BLK
    n = lax.axis_size("ctx")
    assert row_count == BLK and n % 2 == 0
    position = lax.axis_index("ctx").astype(jnp.int32).reshape(1)

    ring = [(i, (i + 2) % n) for i in range(n)]
    mixed = [(i, (i + 3) % n) if i % 2 else (i, i + 1) for i in range(n)]
    swap = [(i, i ^ 1) for i in range(n)]

    ka, va = (lax.ppermute(x, "ctx", ring) for x in (keys, values))
    kc, vc = (lax.ppermute(x, "ctx", mixed) for x in (keys, values))
    kb, vb = (lax.ppermute(x, "ctx", swap) for x in (ka, va))

    acc_shape = jax.ShapeDtypeStruct((groups, rows, 2 * HD), F32)
    shift_shape = jax.ShapeDtypeStruct((groups, rows, HD), BF16)
    work = groups * rows * BLK * HD * 4
    acc, shift = pl.pallas_call(
        functools.partial(own_kernel, groups, size),
        out_shape=(acc_shape, shift_shape),
        in_specs=[VMEM] * 3,
        out_specs=(VMEM, VMEM),
        compiler_params=PARAMS,
        cost_estimate=pl.CostEstimate(flops=work, bytes_accessed=1 << 20, transcendentals=0),
        name="own_block",
    )(queries, keys, values)
    acc = pl.pallas_call(
        functools.partial(add_kernel, groups, size),
        out_shape=acc_shape,
        in_specs=[SMEM, SMEM] + [VMEM] * 5,
        out_specs=VMEM,
        input_output_aliases={6: 0},
        compiler_params=PARAMS,
        cost_estimate=pl.CostEstimate(flops=work, bytes_accessed=1 << 20, transcendentals=0),
        name="second_block",
    )(docs, position, queries, shift, ka, va, acc)
    return pl.pallas_call(
        functools.partial(last_kernel, groups, size),
        out_shape=jax.ShapeDtypeStruct(queries.shape, BF16),
        in_specs=[SMEM, SMEM] + [VMEM] * 7 + [ANY] * 4,
        out_specs=VMEM,
        scratch_shapes=[
            pltpu.VMEM((4, row_count, keys.shape[1]), BF16),
            pltpu.SemaphoreType.DMA((4,)),
        ],
        compiler_params=PARAMS,
        cost_estimate=pl.CostEstimate(flops=2 * work, bytes_accessed=1 << 20, transcendentals=0),
        name="last_blocks",
    )(docs, position, queries, shift, acc, kb, vb, kc, vc, keys, values, ka, va)


def solution(mesh):
    return jax.shard_map(
        on_device,
        mesh=mesh,
        in_specs=(
            P(("seq", "ctx"), None),
            P(("seq", "ctx"), None),
            P(("seq", "ctx"), None),
            P("seq"),
        ),
        out_specs=P(("seq", "ctx"), None),
        check_vma=False,
    )
```

```python
import functools
import math

import jax
import jax.numpy as jnp
from jax import lax
from jax.experimental import pallas as pl
from jax.experimental.pallas import tpu as pltpu
from jax.sharding import PartitionSpec as P

HD = 128
BLK = 128
NEG = -1e30
LOW, HIGH = 1e-25, 1e35
EXP2_SCALE = math.log2(math.e) / math.sqrt(HD)
F32 = jnp.float32
BF16 = jnp.bfloat16
VMEM = pl.BlockSpec(memory_space=pltpu.VMEM)
HBM = pl.BlockSpec(memory_space=pltpu.HBM)
PARAMS = pltpu.CompilerParams(vmem_limit_bytes=40 * 1024 * 1024)


def dot_nt(a, b):
    return lax.dot_general(a, b, (((1,), (1,)), ((), ())), preferred_element_type=F32)


def dot_nn(a, b):
    return lax.dot_general(a, b, (((1,), (0,)), ((), ())), preferred_element_type=F32)


def cut(index, width=HD):
    return slice(index * width, (index + 1) * width)


def group_queries(q_ref, group, size):
    return jnp.concatenate([q_ref[:, cut(group * size + h)] for h in range(size)], axis=0)


def key_head(ref, group):
    return ref[:BLK, cut(group)]


def value_head(ref, group):
    return ref[BLK:, cut(group)]


def penalty(docs_ref, position, distance):
    source = position - distance
    same = docs_ref[jnp.maximum(source, 0)] == docs_ref[position]
    return jnp.where((source >= 0) & same, 0.0, -NEG).astype(F32)


def pack_kernel(k_hbm, v_hbm, kv_ref, sems):
    copies = [
        pltpu.make_async_copy(k_hbm, kv_ref.at[:BLK], sems.at[0]),
        pltpu.make_async_copy(v_hbm, kv_ref.at[BLK:], sems.at[1]),
    ]
    for copy in copies:
        copy.start()
    for copy in copies:
        copy.wait()


def own_kernel(groups, size, docs_hbm, q_hbm, kv_ref, out_ref, total_ref, pen_ref, q_ref, docs_ref, sems):
    copies = [pltpu.make_async_copy(docs_hbm, docs_ref, sems.at[groups])]
    for g in range(groups):
        at = cut(g, size * HD)
        copies.append(pltpu.make_async_copy(q_hbm.at[:, at], q_ref.at[:, at], sems.at[g]))
    for copy in copies[1:] + copies[:1]:
        copy.start()
    row = lax.broadcasted_iota(jnp.int32, (BLK, BLK), 0)
    col = lax.broadcasted_iota(jnp.int32, (BLK, BLK), 1)
    bias = jnp.concatenate([jnp.where(col <= row, 0.0, NEG).astype(F32)] * size, axis=0)
    for g in range(groups):
        copies[1 + g].wait()
        scores = dot_nt(group_queries(q_ref, g, size), key_head(kv_ref, g))
        weights = jnp.exp2(scores * EXP2_SCALE + bias)
        total_ref[g] = weights
        out_ref[g] = dot_nn(weights.astype(BF16), value_head(kv_ref, g))
    copies[0].wait()
    position = lax.axis_index("ctx")
    odd = lax.rem(position, 2)
    for i, distance in enumerate((2, 1, 3)):
        pen_ref[i] = jnp.full((8, HD), penalty(docs_ref, position, distance), F32)


def weigh(scores, pen):
    return jnp.exp2(scores * EXP2_SCALE - pen)


def add_blocks(queries, blocks, pens, group, out, total):
    scores = dot_nt(queries, jnp.concatenate([key_head(x, group) for x in blocks], axis=0))
    weights = [weigh(scores[:, cut(i)], pen) for i, pen in enumerate(pens)]
    rounded = jnp.concatenate([w.astype(BF16) for w in weights], axis=1)
    values = jnp.concatenate([value_head(x, group) for x in blocks], axis=0)
    return out + dot_nn(rounded, values), total + functools.reduce(jnp.add, weights)


def pick(pairs):
    odd = lax.rem(lax.axis_index("ctx"), 2) == 1
    return [jnp.where(odd, y[...], x[...]) for x, y in pairs]


def middle_kernel(groups, size, q_ref, pen_ref, even_a, odd_a, out_in, total_in, out_ref, total_ref):
    blocks = pick([(even_a, odd_a)])
    for g in range(groups):
        out_ref[g], total_ref[g] = add_blocks(
            group_queries(q_ref, g, size), blocks, [pen_ref[0][:1]], g, out_in[g], total_in[g]
        )


def last_kernel(
    groups, size, q_ref, pen_ref, out_in, total_in, even_b, odd_b, even_c, odd_c,
    own_ref, even_a, odd_a, out_hbm, out_ref, low_ref, high_ref, sems,
):
    copies = []
    for g in range(groups):
        at = cut(g, size * HD)
        copies.append(pltpu.make_async_copy(out_ref.at[:, at], out_hbm.at[:, at], sems.at[g]))

    def finish(g, out, total):
        row_total = jnp.sum(total, axis=1, keepdims=True)
        result = (out / row_total).astype(BF16)
        for h in range(size):
            out_ref[:, cut(g * size + h)] = result[cut(h, BLK)]
        copies[g].start()
        return row_total

    def extremes(row_totals):
        low = functools.reduce(jnp.minimum, row_totals)
        high = functools.reduce(jnp.maximum, row_totals)
        low_ref[0] = jnp.min(low)
        high_ref[0] = jnp.max(high)

    first = lax.axis_index("ctx") == 0

    @pl.when(first)
    def _():
        extremes([finish(g, out_in[g], total_in[g]) for g in range(groups)])

    @pl.when(jnp.logical_not(first))
    def _():
        blocks = pick([(even_b, odd_b), (even_c, odd_c)])
        pens = [pen_ref[1][:1], pen_ref[2][:1]]
        extremes([
            finish(g, *add_blocks(group_queries(q_ref, g, size), blocks, pens, g, out_in[g], total_in[g]))
            for g in range(groups)
        ])

    for copy in copies:
        copy.wait()
    safe = (low_ref[0] > LOW) & (high_ref[0] < HIGH)

    @pl.when(jnp.logical_not(safe))
    def _():
        blocks = [own_ref] + pick([(even_a, odd_a), (even_b, odd_b), (even_c, odd_c)])
        row = lax.broadcasted_iota(jnp.int32, (BLK, BLK), 0)
        col = lax.broadcasted_iota(jnp.int32, (BLK, BLK), 1)
        biases = [jnp.where(col <= row, 0.0, NEG).astype(F32)] + [-pen_ref[i][:1] for i in range(3)]
        for g in range(groups):

            def one_head(h, _):
                at = pl.ds(pl.multiple_of((g * size + h) * HD, HD), HD)
                queries = q_ref[:, at]
                scores = [dot_nt(queries, key_head(x, g)) + bias for x, bias in zip(blocks, biases)]
                top = functools.reduce(jnp.maximum, [jnp.max(x, axis=1, keepdims=True) for x in scores])
                weights = [jnp.exp2((x - top) * EXP2_SCALE) for x in scores]
                total = sum(jnp.sum(w, axis=1, keepdims=True) for w in weights)
                product = sum(dot_nn(w.astype(BF16), value_head(x, g)) for w, x in zip(weights, blocks))
                out_ref[:, at] = (product / total).astype(BF16)
                return 0

            lax.fori_loop(0, size, one_head, 0)
        store = pltpu.make_async_copy(out_ref, out_hbm, sems.at[0])
        store.start()
        store.wait()


def routes(n):
    step = n // 4
    forward = []
    for parity in (0, 1):
        route = {i: i + 2 for i in range(parity, n - 2, 2)}
        last = n - 2 + parity
        chain = [last, last ^ 1] + [(last ^ 1) - step * k for k in range(1, 4)] + [parity]
        route.update(zip(chain, chain[1:]))
        route.update({i: i ^ step for i in range(1 - parity, n, 2) if i not in route})
        forward.append(sorted(route.items()))
    across = {i: i + 3 for i in range(1, n - 3, 2)}
    for start, end in ((n - 3, 0), (n - 1, 2)):
        at = start
        for k in range(3):
            across[at] = start - step * (k + 1)
            at = across[at] - 1
        across[at] = end
    across.update({i: i + 1 for i in range(0, n, 2) if i not in across})
    swap = [(i, i ^ 1) for i in range(n)]
    return forward[0], forward[1], sorted(across.items()), swap


def in_hbm(array):
    return pltpu.with_memory_space_constraint(array, pltpu.HBM)


def after(value, *others):
    return lax.optimization_barrier((value, *others))[0]


def on_device(queries, keys, values, docs):
    row_count, width = keys.shape
    groups = width // HD
    size = queries.shape[1] // width
    rows = size * BLK
    n = lax.axis_size("ctx")
    assert row_count == BLK and n % 8 == 0
    even_on, odd_on, across, swap = routes(n)
    work = groups * rows * BLK * HD * 4
    cost = pl.CostEstimate(flops=0, bytes_accessed=0, transcendentals=0)
    packed = jax.ShapeDtypeStruct((2 * BLK, width), BF16)
    running = jax.ShapeDtypeStruct((groups, rows, HD), F32)
    dma = pltpu.SemaphoreType.DMA

    def move(block, route):
        return lax.ppermute(block, "ctx", route)

    def own(block):
        return pl.pallas_call(
            functools.partial(own_kernel, groups, size),
            out_shape=(running,) * 2 + (jax.ShapeDtypeStruct((3, 8, HD), F32), jax.ShapeDtypeStruct(queries.shape, BF16)),
            in_specs=[HBM, HBM, VMEM],
            out_specs=(VMEM,) * 4,
            scratch_shapes=[pltpu.SMEM(docs.shape, jnp.int32), dma((groups + 1,))],
            compiler_params=PARAMS,
            cost_estimate=cost,
            name="own_block",
        )(in_hbm(docs), in_hbm(queries), block)

    block = pl.pallas_call(
        pack_kernel,
        out_shape=packed,
        in_specs=[HBM, HBM],
        out_specs=VMEM,
        scratch_shapes=[dma((2,))],
        compiler_params=PARAMS,
        name="pack",
    )(in_hbm(keys), in_hbm(values))
    odd_a = move(block, odd_on)
    even_a = move(block, even_on)
    odd_b = move(block, swap)
    out, total, pen, local = own(block)
    even_c = move(after(block, pen), across)
    even_b = move(after(odd_a, pen), swap)
    odd_c = move(after(even_a, pen), swap)
    out, total = pl.pallas_call(
        functools.partial(middle_kernel, groups, size),
        out_shape=(running,) * 2,
        in_specs=[VMEM] * 6,
        out_specs=(VMEM,) * 2,
        input_output_aliases={4: 0, 5: 1},
        compiler_params=PARAMS,
        cost_estimate=cost,
        name="middle_block",
    )(local, pen, even_a, odd_a, out, total)
    return pl.pallas_call(
        functools.partial(last_kernel, groups, size),
        out_shape=jax.ShapeDtypeStruct(queries.shape, BF16),
        in_specs=[VMEM] * 11,
        out_specs=HBM,
        scratch_shapes=[
            pltpu.VMEM(queries.shape, BF16),
            pltpu.SMEM((1,), F32),
            pltpu.SMEM((1,), F32),
            dma((groups,)),
        ],
        compiler_params=PARAMS,
        cost_estimate=cost,
        name="last_blocks",
    )(local, pen, out, total, even_b, odd_b, even_c, odd_c, block, even_a, odd_a)


def solution(mesh):
    return jax.shard_map(
        on_device,
        mesh=mesh,
        in_specs=(
            P(("seq", "ctx"), None),
            P(("seq", "ctx"), None),
            P(("seq", "ctx"), None),
            P("seq"),
        ),
        out_specs=P(("seq", "ctx"), None),
        check_vma=False,
    )
```

```python
import functools
import math

import jax
import jax.numpy as jnp
from jax import lax
from jax.experimental import pallas as pl
from jax.experimental.pallas import tpu as pltpu
from jax.sharding import PartitionSpec as P

HD = 128
BLK = 128
NEG = -1e30
LOW, HIGH = 1e-25, 1e35
EXP2_SCALE = math.log2(math.e) / math.sqrt(HD)
F32 = jnp.float32
BF16 = jnp.bfloat16
VMEM = pl.BlockSpec(memory_space=pltpu.VMEM)
HBM = pl.BlockSpec(memory_space=pltpu.HBM)
PARAMS = pltpu.CompilerParams(vmem_limit_bytes=40 * 1024 * 1024)


def dot_nt(a, b):
    return lax.dot_general(a, b, (((1,), (1,)), ((), ())), preferred_element_type=F32)


def dot_nn(a, b):
    return lax.dot_general(a, b, (((1,), (0,)), ((), ())), preferred_element_type=F32)


def cut(index, width=HD):
    return slice(index * width, (index + 1) * width)


def group_queries(q_ref, group, size):
    return jnp.concatenate([q_ref[:, cut(group * size + h)] for h in range(size)], axis=0)


def key_head(ref, group):
    return ref[:BLK, cut(group)]


def value_head(ref, group):
    return ref[BLK:, cut(group)]


def penalty(docs_ref, position, distance):
    source = position - distance
    same = docs_ref[jnp.maximum(source, 0)] == docs_ref[position]
    return jnp.where((source >= 0) & same, 0.0, -NEG).astype(F32)


def pack_kernel(k_hbm, v_hbm, kv_ref, sems):
    copies = [
        pltpu.make_async_copy(k_hbm, kv_ref.at[:BLK], sems.at[0]),
        pltpu.make_async_copy(v_hbm, kv_ref.at[BLK:], sems.at[1]),
    ]
    for copy in copies:
        copy.start()
    for copy in copies:
        copy.wait()


def load_queries(groups, size, q_hbm, q_ref, sems):
    spans = [cut(g, size * HD) for g in range(groups)]
    return [pltpu.make_async_copy(q_hbm.at[:, at], q_ref.at[:, at], sems.at[g]) for g, at in enumerate(spans)]


def own_blocks(size, some, q_ref, kv_ref, out_ref, total_ref, before=lambda g: None):
    row = lax.broadcasted_iota(jnp.int32, (BLK, BLK), 0)
    col = lax.broadcasted_iota(jnp.int32, (BLK, BLK), 1)
    bias = jnp.concatenate([jnp.where(col <= row, 0.0, NEG).astype(F32)] * size, axis=0)
    for g in some:
        before(g)
        scores = dot_nt(group_queries(q_ref, g, size), key_head(kv_ref, g))
        weights = jnp.exp2(scores * EXP2_SCALE + bias)
        total_ref[g] = weights
        out_ref[g] = dot_nn(weights.astype(BF16), value_head(kv_ref, g))


def own_kernel(groups, size, some, docs_hbm, q_hbm, kv_ref, out_ref, total_ref, pen_ref, q_ref, docs_ref, sems):
    docs_copy = pltpu.make_async_copy(docs_hbm, docs_ref, sems.at[groups])
    copies = load_queries(groups, size, q_hbm, q_ref, sems)
    for copy in copies + [docs_copy]:
        copy.start()
    own_blocks(size, some, q_ref, kv_ref, out_ref, total_ref, lambda g: copies[g].wait())
    for g in range(groups):
        if g not in some:
            copies[g].wait()
    docs_copy.wait()
    for i, distance in enumerate((2, 1, 3)):
        pen_ref[i] = jnp.full((8, HD), penalty(docs_ref, lax.axis_index("ctx"), distance), F32)


def rest_kernel(size, some, q_ref, kv_ref, out_in, total_in, out_ref, total_ref):
    own_blocks(size, some, q_ref, kv_ref, out_ref, total_ref)


def weigh(scores, pen):
    return jnp.exp2(scores * EXP2_SCALE - pen)


def add_blocks(queries, blocks, pens, group, out, total):
    scores = dot_nt(queries, jnp.concatenate([key_head(x, group) for x in blocks], axis=0))
    weights = [weigh(scores[:, cut(i)], pen) for i, pen in enumerate(pens)]
    rounded = jnp.concatenate([w.astype(BF16) for w in weights], axis=1)
    values = jnp.concatenate([value_head(x, group) for x in blocks], axis=0)
    return out + dot_nn(rounded, values), total + functools.reduce(jnp.add, weights)


def add_kernel(groups, size, q_ref, pen_ref, odd_a, out_in, total_in, out_ref, total_ref):
    @pl.when(lax.rem(lax.axis_index("ctx"), 2) == 1)
    def _():
        for g in range(groups):
            out_ref[g], total_ref[g] = add_blocks(
                group_queries(q_ref, g, size), [odd_a], [pen_ref[0][:1]], g, out_in[g], total_in[g]
            )


def finish(size, g, out, total, result_ref):
    row_total = jnp.sum(total, axis=1, keepdims=True)
    result = (out / row_total).astype(BF16)
    for h in range(size):
        result_ref[:, cut(g * size + h)] = result[cut(h, BLK)]
    return row_total


def note_extremes(row_totals, range_ref):
    low = functools.reduce(jnp.minimum, row_totals)
    high = functools.reduce(jnp.maximum, row_totals)
    range_ref[0] = jnp.full((8, HD), jnp.min(low), F32)
    range_ref[1] = jnp.full((8, HD), jnp.max(high), F32)


def even_kernel(groups, size, q_ref, pen_ref, even_a, even_b, out_in, total_in, out_ref, total_ref, out_hbm, range_ref, result_ref, sem):
    position = lax.axis_index("ctx")
    range_ref[...] = jnp.ones_like(range_ref)

    @pl.when((lax.rem(position, 2) == 0) & (position > 0))
    def _():
        pens = [pen_ref[i][:1] for i in (0, 1)]
        for g in range(groups):
            out_ref[g], total_ref[g] = add_blocks(
                group_queries(q_ref, g, size), [even_a, even_b], pens, g, out_in[g], total_in[g]
            )

    @pl.when(position == 0)
    def _():
        note_extremes([finish(size, g, out_in[g], total_in[g], result_ref) for g in range(groups)], range_ref)
        copy = pltpu.make_async_copy(result_ref, out_hbm, sem)
        copy.start()
        copy.wait()


def last_kernel(
    groups, size, q_ref, pen_ref, out_in, total_in, odd_b, odd_c, even_c,
    own_ref, even_a, odd_a, even_b, early_range, _, out_hbm, result_ref, range_ref, sems,
):
    position = lax.axis_index("ctx")
    odd = lax.rem(position, 2) == 1
    copies = []
    for g in range(groups):
        at = cut(g, size * HD)
        copies.append(pltpu.make_async_copy(result_ref.at[:, at], out_hbm.at[:, at], sems.at[g]))
    range_ref[...] = early_range[...]

    def whole(blocks, indices):
        pens = [pen_ref[i][:1] for i in indices]
        row_totals = []
        for g in range(groups):
            out, total = add_blocks(group_queries(q_ref, g, size), blocks, pens, g, out_in[g], total_in[g])
            row_totals.append(finish(size, g, out, total, result_ref))
            copies[g].start()
        note_extremes(row_totals, range_ref)

    @pl.when(jnp.logical_not(odd) & (position > 0))
    def _():
        whole([even_c], [2])

    @pl.when(odd)
    def _():
        whole([odd_b, odd_c], [1, 2])

    safe = (jnp.min(range_ref[0]) > LOW) & (jnp.max(range_ref[1]) < HIGH)

    @pl.when(position > 0)
    def _():
        for copy in copies:
            copy.wait()

    @pl.when(jnp.logical_not(safe))
    def _():
        row = lax.broadcasted_iota(jnp.int32, (BLK, BLK), 0)
        col = lax.broadcasted_iota(jnp.int32, (BLK, BLK), 1)
        biases = [jnp.where(col <= row, 0.0, NEG).astype(F32)] + [-pen_ref[i][:1] for i in range(3)]
        pairs = ((even_a, odd_a), (even_b, odd_b), (even_c, odd_c))
        for g in range(groups):
            keys, values = (
                [part(own_ref, g)] + [jnp.where(odd, part(y, g), part(x, g)) for x, y in pairs]
                for part in (key_head, value_head)
            )

            def one_head(h, _):
                at = pl.ds(pl.multiple_of((g * size + h) * HD, HD), HD)
                queries = q_ref[:, at]
                scores = [dot_nt(queries, x) + bias for x, bias in zip(keys, biases)]
                top = functools.reduce(jnp.maximum, [jnp.max(x, axis=1, keepdims=True) for x in scores])
                weights = [jnp.exp2((x - top) * EXP2_SCALE) for x in scores]
                total = sum(jnp.sum(w, axis=1, keepdims=True) for w in weights)
                product = sum(dot_nn(w.astype(BF16), x) for w, x in zip(weights, values))
                result_ref[:, at] = (product / total).astype(BF16)
                return 0

            lax.fori_loop(0, size, one_head, 0)
        store = pltpu.make_async_copy(result_ref, out_hbm, sems.at[0])
        store.start()
        store.wait()


def routes(n):
    step = n // 4
    forward = []
    for parity in (0, 1):
        route = {i: i + 2 for i in range(parity, n - 2, 2)}
        last = n - 2 + parity
        chain = [last, last ^ 1] + [(last ^ 1) - step * k for k in range(1, 4)] + [parity]
        route.update(zip(chain, chain[1:]))
        route.update({i: i ^ step for i in range(1 - parity, n, 2) if i not in route})
        forward.append(sorted(route.items()))
    across = {i: i + 3 for i in range(1, n - 3, 2)}
    for start, end in ((n - 3, 0), (n - 1, 2)):
        at = start
        for place in [start - step * (k + 1) for k in range(3)] + [end]:
            across[at] = place
            at = place - 1
    across.update({i: i + 1 for i in range(0, n, 2) if i not in across})
    swap = [(i, i ^ 1) for i in range(n)]
    return forward[0], forward[1], sorted(across.items()), swap


def in_hbm(array):
    return pltpu.with_memory_space_constraint(array, pltpu.HBM)


def after(value, *others):
    return lax.optimization_barrier((value, *others))[0]


def on_device(queries, keys, values, docs):
    row_count, width = keys.shape
    groups = width // HD
    size = queries.shape[1] // width
    rows = size * BLK
    n = lax.axis_size("ctx")
    assert row_count == BLK and n % 8 == 0
    even_on, odd_on, across, swap = routes(n)
    work = groups * rows * BLK * HD * 4
    cost = pl.CostEstimate(flops=0, bytes_accessed=0, transcendentals=0)
    packed = jax.ShapeDtypeStruct((2 * BLK, width), BF16)
    running = jax.ShapeDtypeStruct((groups, rows, HD), F32)
    extremes = jax.ShapeDtypeStruct((2, 8, HD), F32)
    result = jax.ShapeDtypeStruct(queries.shape, BF16)
    dma = pltpu.SemaphoreType.DMA

    def move(block, route):
        return lax.ppermute(block, "ctx", route)

    def own(block):
        some = tuple(range(groups))[:4]
        return pl.pallas_call(
            functools.partial(own_kernel, groups, size, some),
            out_shape=(running,) * 2 + (jax.ShapeDtypeStruct((3, 8, HD), F32), jax.ShapeDtypeStruct(queries.shape, BF16)),
            in_specs=[HBM, HBM, VMEM],
            out_specs=(VMEM,) * 4,
            scratch_shapes=[pltpu.SMEM(docs.shape, jnp.int32), dma((groups + 1,))],
            compiler_params=PARAMS,
            cost_estimate=cost,
            name="own_block",
        )(in_hbm(docs), in_hbm(queries), block)

    def rest(local, block, out, total):
        some = tuple(range(groups))[4:]
        return pl.pallas_call(
            functools.partial(rest_kernel, size, some),
            out_shape=(running,) * 2,
            in_specs=[VMEM] * 4,
            out_specs=(VMEM,) * 2,
            input_output_aliases={2: 0, 3: 1},
            compiler_params=PARAMS,
            cost_estimate=cost,
            name="own_rest",
        )(local, block, out, total)

    def add_odd(local, pen, out, total, odd_a):
        return pl.pallas_call(
            functools.partial(add_kernel, groups, size),
            out_shape=(running,) * 2,
            in_specs=[VMEM] * 5,
            out_specs=(VMEM,) * 2,
            input_output_aliases={3: 0, 4: 1},
            compiler_params=PARAMS,
            cost_estimate=cost,
            name="odd_blocks",
        )(local, pen, odd_a, out, total)

    def add_even(local, pen, out, total, even_a, even_b):
        return pl.pallas_call(
            functools.partial(even_kernel, groups, size),
            out_shape=(running, running, result, extremes),
            in_specs=[VMEM] * 6,
            out_specs=(VMEM, VMEM, HBM, VMEM),
            input_output_aliases={4: 0, 5: 1},
            scratch_shapes=[pltpu.VMEM(result.shape, BF16), dma(())],
            compiler_params=PARAMS,
            cost_estimate=cost,
            name="even_blocks",
        )(local, pen, even_a, even_b, out, total)

    block = pl.pallas_call(
        pack_kernel,
        out_shape=packed,
        in_specs=[HBM, HBM],
        out_specs=VMEM,
        scratch_shapes=[dma((2,))],
        compiler_params=PARAMS,
        name="pack",
    )(in_hbm(keys), in_hbm(values))
    odd_a = move(block, odd_on)
    even_a = move(block, even_on)
    out, total, pen, local = own(block)
    even_c = move(after(block, pen), across)
    odd_b = move(after(block, pen), swap)
    out, total = add_odd(local, pen, out, total, odd_a)
    even_b = move(after(odd_a, out), swap)
    odd_c = move(after(even_a, out), swap)
    out, total, early, early_range = add_even(local, pen, out, total, even_a, even_b)
    return pl.pallas_call(
        functools.partial(last_kernel, groups, size),
        out_shape=result,
        in_specs=[VMEM] * 12 + [HBM],
        out_specs=HBM,
        input_output_aliases={12: 0},
        scratch_shapes=[pltpu.VMEM(result.shape, BF16), pltpu.VMEM(extremes.shape, F32), dma((groups,))],
        compiler_params=PARAMS,
        cost_estimate=cost,
        name="last_blocks",
    )(
        local, pen, out, total, odd_b, odd_c, even_c, block, even_a, odd_a, even_b,
        early_range, in_hbm(early),
    )


def solution(mesh):
    return jax.shard_map(
        on_device,
        mesh=mesh,
        in_specs=(
            P(("seq", "ctx"), None),
            P(("seq", "ctx"), None),
            P(("seq", "ctx"), None),
            P("seq"),
        ),
        out_specs=P(("seq", "ctx"), None),
        check_vma=False,
    )
```

```python
import functools
import math

import jax
import jax.numpy as jnp
from jax import lax
from jax.experimental import pallas as pl
from jax.experimental.pallas import tpu as pltpu
from jax.sharding import PartitionSpec as P

HD = 128
BLK = 128
NEG = -1e30
LOW, HIGH = 1e-25, 1e35
EXP2_SCALE = math.log2(math.e) / math.sqrt(HD)
OWN_UNIT, ADD_UNIT, LAST_UNIT, PACK_PARTS = 8, 8, 4, 4
F32 = jnp.float32
BF16 = jnp.bfloat16
VMEM = pl.BlockSpec(memory_space=pltpu.VMEM)
HBM = pl.BlockSpec(memory_space=pltpu.HBM)
PARAMS = pltpu.CompilerParams(vmem_limit_bytes=40 * 1024 * 1024)


def dot_nt(a, b):
    return lax.dot_general(a, b, (((1,), (1,)), ((), ())), preferred_element_type=F32)


def dot_nn(a, b):
    return lax.dot_general(a, b, (((1,), (0,)), ((), ())), preferred_element_type=F32)


def cut(index, width=HD):
    return slice(index * width, (index + 1) * width)


def unit_queries(q_ref, size, unit):
    g, first, count = unit
    return jnp.concatenate([q_ref[:, cut(g * size + first + h)] for h in range(count)], axis=0)


def unit_rows(unit):
    return slice(unit[1] * BLK, (unit[1] + unit[2]) * BLK)


def units_of(groups, size, count):
    return [(g, first, count) for g in groups for first in range(0, size, count)]


def in_turn(units, first, second):
    for unit in units:
        second(unit, first(unit))


def staggered(units, first, second):
    waiting = None
    for unit in units:
        ready = (unit, first(unit))
        if waiting is not None:
            second(*waiting)
        waiting = ready
    second(*waiting)


def key_head(ref, group):
    return ref[:BLK, cut(group)]


def value_head(ref, group):
    return ref[BLK:, cut(group)]


def penalty(docs_ref, position, distance):
    source = position - distance
    same = docs_ref[jnp.maximum(source, 0)] == docs_ref[position]
    return jnp.where((source >= 0) & same, 0.0, -NEG).astype(F32)


def pack_kernel(k_hbm, v_hbm, kv_ref, sems):
    copies = []
    for first, hbm in ((0, k_hbm), (BLK, v_hbm)):
        for part in range(PACK_PARTS):
            rows = BLK // PACK_PARTS
            source = hbm.at[cut(part, rows)]
            target = kv_ref.at[pl.ds(first + part * rows, rows)]
            copies.append(pltpu.make_async_copy(source, target, sems.at[len(copies)]))
    for copy in copies:
        copy.start()
    for copy in copies:
        copy.wait()


def load_queries(groups, size, q_hbm, q_ref, sems):
    spans = [cut(g, size * HD) for g in range(groups)]
    return [pltpu.make_async_copy(q_hbm.at[:, at], q_ref.at[:, at], sems.at[g]) for g, at in enumerate(spans)]


def own_blocks(size, some, q_ref, kv_ref, out_ref, total_ref, before=lambda g: None):
    row = lax.broadcasted_iota(jnp.int32, (BLK, BLK), 0)
    col = lax.broadcasted_iota(jnp.int32, (BLK, BLK), 1)
    count = OWN_UNIT
    bias = jnp.concatenate([jnp.where(col <= row, 0.0, NEG).astype(F32)] * count, axis=0)

    def first(unit):
        if unit[1] == 0:
            before(unit[0])
        scores = dot_nt(unit_queries(q_ref, size, unit), key_head(kv_ref, unit[0]))
        return jnp.exp2(scores * EXP2_SCALE + bias)

    def second(unit, weights):
        g, rows = unit[0], unit_rows(unit)
        total_ref[g, rows] = weights
        out_ref[g, rows] = dot_nn(weights.astype(BF16), value_head(kv_ref, g))

    staggered(units_of(some, size, count), first, second)


def own_kernel(groups, size, some, docs_hbm, q_hbm, kv_ref, out_ref, total_ref, pen_ref, q_ref, docs_ref, sems):
    docs_copy = pltpu.make_async_copy(docs_hbm, docs_ref, sems.at[groups])
    copies = load_queries(groups, size, q_hbm, q_ref, sems)
    for copy in copies + [docs_copy]:
        copy.start()
    own_blocks(size, some, q_ref, kv_ref, out_ref, total_ref, lambda g: copies[g].wait())
    for g in range(groups):
        if g not in some:
            copies[g].wait()
    docs_copy.wait()
    for i, distance in enumerate((2, 1, 3)):
        pen_ref[i] = jnp.full((8, HD), penalty(docs_ref, lax.axis_index("ctx"), distance), F32)


def rest_kernel(size, some, q_ref, kv_ref, out_in, total_in, out_ref, total_ref):
    own_blocks(size, some, q_ref, kv_ref, out_ref, total_ref)


def weigh(scores, pen):
    return jnp.exp2(scores * EXP2_SCALE - pen)


def add_blocks(run, groups, size, count, q_ref, blocks, pens, out_in, total_in, store):
    def first(unit):
        keys = jnp.concatenate([key_head(x, unit[0]) for x in blocks], axis=0)
        scores = dot_nt(unit_queries(q_ref, size, unit), keys)
        return [weigh(scores[:, cut(i)], pen) for i, pen in enumerate(pens)]

    def second(unit, weights):
        g, rows = unit[0], unit_rows(unit)
        rounded = jnp.concatenate([w.astype(BF16) for w in weights], axis=1)
        values = jnp.concatenate([value_head(x, g) for x in blocks], axis=0)
        out = out_in[g, rows] + dot_nn(rounded, values)
        store(unit, out, total_in[g, rows] + functools.reduce(jnp.add, weights))

    run(units_of(range(groups), size, count), first, second)


def keep(out_ref, total_ref):
    def store(unit, out, total):
        out_ref[unit[0], unit_rows(unit)] = out
        total_ref[unit[0], unit_rows(unit)] = total

    return store


def add_kernel(groups, size, q_ref, pen_ref, odd_a, out_in, total_in, out_ref, total_ref):
    @pl.when(lax.rem(lax.axis_index("ctx"), 2) == 1)
    def _():
        pens = [pen_ref[0][:1]]
        add_blocks(in_turn, groups, size, ADD_UNIT, q_ref, [odd_a], pens, out_in, total_in, keep(out_ref, total_ref))


def finish(size, unit, out, total, result_ref):
    row_total = jnp.sum(total, axis=1, keepdims=True)
    result = (out / row_total).astype(BF16)
    g, first, count = unit
    for h in range(count):
        result_ref[:, cut(g * size + first + h)] = result[cut(h, BLK)]
    return row_total


def note_extremes(row_totals, range_ref):
    low = functools.reduce(jnp.minimum, row_totals)
    high = functools.reduce(jnp.maximum, row_totals)
    range_ref[0] = jnp.full((8, HD), jnp.min(low), F32)
    range_ref[1] = jnp.full((8, HD), jnp.max(high), F32)


def even_kernel(groups, size, q_ref, pen_ref, even_a, even_b, out_in, total_in, out_ref, total_ref, out_hbm, range_ref, result_ref, sem):
    position = lax.axis_index("ctx")
    range_ref[...] = jnp.ones_like(range_ref)

    @pl.when((lax.rem(position, 2) == 0) & (position > 0))
    def _():
        pens = [pen_ref[i][:1] for i in (0, 1)]
        add_blocks(in_turn, groups, size, ADD_UNIT, q_ref, [even_a, even_b], pens, out_in, total_in, keep(out_ref, total_ref))

    @pl.when(position == 0)
    def _():
        whole = units_of(range(groups), size, size)
        note_extremes([finish(size, u, out_in[u[0]], total_in[u[0]], result_ref) for u in whole], range_ref)
        copy = pltpu.make_async_copy(result_ref, out_hbm, sem)
        copy.start()
        copy.wait()


def last_kernel(
    groups, size, q_ref, pen_ref, out_in, total_in, odd_b, odd_c, even_c,
    own_ref, even_a, odd_a, even_b, early_range, _, out_hbm, result_ref, range_ref, sems,
):
    position = lax.axis_index("ctx")
    odd = lax.rem(position, 2) == 1
    units = units_of(range(groups), size, LAST_UNIT)
    copies = {}
    for n, unit in enumerate(units):
        start = (unit[0] * size + unit[1]) * HD
        at = slice(start, start + unit[2] * HD)
        copies[unit] = pltpu.make_async_copy(result_ref.at[:, at], out_hbm.at[:, at], sems.at[n])
    range_ref[...] = early_range[...]

    def whole(blocks, indices):
        pens = [pen_ref[i][:1] for i in indices]
        row_totals = []

        def store(unit, out, total):
            row_totals.append(finish(size, unit, out, total, result_ref))
            copies[unit].start()

        add_blocks(staggered, groups, size, LAST_UNIT, q_ref, blocks, pens, out_in, total_in, store)
        note_extremes(row_totals, range_ref)

    @pl.when(jnp.logical_not(odd) & (position > 0))
    def _():
        whole([even_c], [2])

    @pl.when(odd)
    def _():
        whole([odd_b, odd_c], [1, 2])

    safe = (jnp.min(range_ref[0]) > LOW) & (jnp.max(range_ref[1]) < HIGH)

    @pl.when(position > 0)
    def _():
        for copy in copies.values():
            copy.wait()

    @pl.when(jnp.logical_not(safe))
    def _():
        row = lax.broadcasted_iota(jnp.int32, (BLK, BLK), 0)
        col = lax.broadcasted_iota(jnp.int32, (BLK, BLK), 1)
        biases = [jnp.where(col <= row, 0.0, NEG).astype(F32)] + [-pen_ref[i][:1] for i in range(3)]
        pairs = ((even_a, odd_a), (even_b, odd_b), (even_c, odd_c))
        for g in range(groups):
            keys, values = (
                [part(own_ref, g)] + [jnp.where(odd, part(y, g), part(x, g)) for x, y in pairs]
                for part in (key_head, value_head)
            )

            def one_head(h, _):
                at = pl.ds(pl.multiple_of((g * size + h) * HD, HD), HD)
                queries = q_ref[:, at]
                scores = [dot_nt(queries, x) + bias for x, bias in zip(keys, biases)]
                top = functools.reduce(jnp.maximum, [jnp.max(x, axis=1, keepdims=True) for x in scores])
                weights = [jnp.exp2((x - top) * EXP2_SCALE) for x in scores]
                total = sum(jnp.sum(w, axis=1, keepdims=True) for w in weights)
                product = sum(dot_nn(w.astype(BF16), x) for w, x in zip(weights, values))
                result_ref[:, at] = (product / total).astype(BF16)
                return 0

            lax.fori_loop(0, size, one_head, 0)
        store = pltpu.make_async_copy(result_ref, out_hbm, sems.at[0])
        store.start()
        store.wait()


def routes(n):
    step = n // 4
    forward = []
    for parity in (0, 1):
        route = {i: i + 2 for i in range(parity, n - 2, 2)}
        last = n - 2 + parity
        chain = [last, last ^ 1] + [(last ^ 1) - step * k for k in range(1, 4)] + [parity]
        route.update(zip(chain, chain[1:]))
        route.update({i: i ^ step for i in range(1 - parity, n, 2) if i not in route})
        forward.append(sorted(route.items()))
    across = {i: i + 3 for i in range(1, n - 3, 2)}
    for start, end in ((n - 3, 0), (n - 1, 2)):
        at = start
        for place in [start - step * (k + 1) for k in range(3)] + [end]:
            across[at] = place
            at = place - 1
    across.update({i: i + 1 for i in range(0, n, 2) if i not in across})
    swap = [(i, i ^ 1) for i in range(n)]
    return forward[0], forward[1], sorted(across.items()), swap


def in_hbm(array):
    return pltpu.with_memory_space_constraint(array, pltpu.HBM)


def after(value, *others):
    return lax.optimization_barrier((value, *others))[0]


def on_device(queries, keys, values, docs):
    row_count, width = keys.shape
    groups = width // HD
    size = queries.shape[1] // width
    rows = size * BLK
    n = lax.axis_size("ctx")
    assert row_count == BLK and n % 8 == 0
    even_on, odd_on, across, swap = routes(n)
    work = groups * rows * BLK * HD * 4
    cost = pl.CostEstimate(flops=0, bytes_accessed=0, transcendentals=0)
    packed = jax.ShapeDtypeStruct((2 * BLK, width), BF16)
    running = jax.ShapeDtypeStruct((groups, rows, HD), F32)
    extremes = jax.ShapeDtypeStruct((2, 8, HD), F32)
    result = jax.ShapeDtypeStruct(queries.shape, BF16)
    dma = pltpu.SemaphoreType.DMA

    def move(block, route):
        return lax.ppermute(block, "ctx", route)

    def own(block):
        some = tuple(range(groups))[:4]
        return pl.pallas_call(
            functools.partial(own_kernel, groups, size, some),
            out_shape=(running,) * 2 + (jax.ShapeDtypeStruct((3, 8, HD), F32), jax.ShapeDtypeStruct(queries.shape, BF16)),
            in_specs=[HBM, HBM, VMEM],
            out_specs=(VMEM,) * 4,
            scratch_shapes=[pltpu.SMEM(docs.shape, jnp.int32), dma((groups + 1,))],
            compiler_params=PARAMS,
            cost_estimate=cost,
            name="own_block",
        )(in_hbm(docs), in_hbm(queries), block)

    def rest(local, block, out, total):
        some = tuple(range(groups))[4:]
        return pl.pallas_call(
            functools.partial(rest_kernel, size, some),
            out_shape=(running,) * 2,
            in_specs=[VMEM] * 4,
            out_specs=(VMEM,) * 2,
            input_output_aliases={2: 0, 3: 1},
            compiler_params=PARAMS,
            cost_estimate=cost,
            name="own_rest",
        )(local, block, out, total)

    def add_odd(local, pen, out, total, odd_a):
        return pl.pallas_call(
            functools.partial(add_kernel, groups, size),
            out_shape=(running,) * 2,
            in_specs=[VMEM] * 5,
            out_specs=(VMEM,) * 2,
            input_output_aliases={3: 0, 4: 1},
            compiler_params=PARAMS,
            cost_estimate=cost,
            name="odd_blocks",
        )(local, pen, odd_a, out, total)

    def add_even(local, pen, out, total, even_a, even_b):
        return pl.pallas_call(
            functools.partial(even_kernel, groups, size),
            out_shape=(running, running, result, extremes),
            in_specs=[VMEM] * 6,
            out_specs=(VMEM, VMEM, HBM, VMEM),
            input_output_aliases={4: 0, 5: 1},
            scratch_shapes=[pltpu.VMEM(result.shape, BF16), dma(())],
            compiler_params=PARAMS,
            cost_estimate=cost,
            name="even_blocks",
        )(local, pen, even_a, even_b, out, total)

    block = pl.pallas_call(
        pack_kernel,
        out_shape=packed,
        in_specs=[HBM, HBM],
        out_specs=VMEM,
        scratch_shapes=[dma((2 * PACK_PARTS,))],
        compiler_params=PARAMS,
        name="pack",
    )(in_hbm(keys), in_hbm(values))
    odd_a = move(block, odd_on)
    even_a = move(block, even_on)
    out, total, pen, local = own(block)
    even_c = move(after(block, pen), across)
    odd_b = move(after(block, pen), swap)
    out, total = add_odd(local, pen, out, total, odd_a)
    even_b = move(after(odd_a, out), swap)
    odd_c = move(after(even_a, out), swap)
    out, total, early, early_range = add_even(local, pen, out, total, even_a, even_b)
    return pl.pallas_call(
        functools.partial(last_kernel, groups, size),
        out_shape=result,
        in_specs=[VMEM] * 12 + [HBM],
        out_specs=HBM,
        input_output_aliases={12: 0},
        scratch_shapes=[pltpu.VMEM(result.shape, BF16), pltpu.VMEM(extremes.shape, F32), dma((groups * size // LAST_UNIT,))],
        compiler_params=PARAMS,
        cost_estimate=cost,
        name="last_blocks",
    )(
        local, pen, out, total, odd_b, odd_c, even_c, block, even_a, odd_a, even_b,
        early_range, in_hbm(early),
    )


def solution(mesh):
    return jax.shard_map(
        on_device,
        mesh=mesh,
        in_specs=(
            P(("seq", "ctx"), None),
            P(("seq", "ctx"), None),
            P(("seq", "ctx"), None),
            P("seq"),
        ),
        out_specs=P(("seq", "ctx"), None),
        check_vma=False,
    )
```

```python
import functools
import math

import jax
import jax.numpy as jnp
from jax import lax
from jax.experimental import pallas as pl
from jax.experimental.pallas import tpu as pltpu
from jax.sharding import PartitionSpec as P

HD = 128
BLK = 128
NEG = -1e30
LOW, HIGH = 1e-25, 1e35
EXP2_SCALE = math.log2(math.e) / math.sqrt(HD)
OWN_UNIT, ADD_UNIT, LAST_UNIT = 8, 8, 4
F32 = jnp.float32
BF16 = jnp.bfloat16
VMEM = pl.BlockSpec(memory_space=pltpu.VMEM)
HBM = pl.BlockSpec(memory_space=pltpu.HBM)
PARAMS = pltpu.CompilerParams(vmem_limit_bytes=40 * 1024 * 1024)


def dot_nt(a, b):
    return lax.dot_general(a, b, (((1,), (1,)), ((), ())), preferred_element_type=F32)


def dot_nn(a, b):
    return lax.dot_general(a, b, (((1,), (0,)), ((), ())), preferred_element_type=F32)


def cut(index, width=HD):
    return slice(index * width, (index + 1) * width)


def with_ones(values):
    return jnp.concatenate([values, jnp.ones_like(values)], axis=1)


def unit_queries(q_ref, size, unit):
    g, first, count = unit
    return jnp.concatenate([q_ref[:, cut(g * size + first + h)] for h in range(count)], axis=0)


def unit_rows(unit):
    return slice(unit[1] * BLK, (unit[1] + unit[2]) * BLK)


def units_of(groups, size, count):
    return [(g, first, count) for g in range(groups) for first in range(0, size, count)]


def staggered(units, first, second):
    waiting = None
    for unit in units:
        ready = (unit, first(unit))
        if waiting is not None:
            second(*waiting)
        waiting = ready
    second(*waiting)


def penalty(docs_ref, position, distance):
    source = position - distance
    same = docs_ref[jnp.maximum(source, 0)] == docs_ref[position]
    return jnp.where((source >= 0) & same, 0.0, -NEG).astype(F32)


def weigh(scores, pen):
    return jnp.exp2(scores * EXP2_SCALE - pen).astype(BF16)


def causal_pen():
    row = lax.broadcasted_iota(jnp.int32, (BLK, BLK), 0)
    col = lax.broadcasted_iota(jnp.int32, (BLK, BLK), 1)
    return jnp.where(col <= row, 0.0, -NEG).astype(F32)


def own_kernel(groups, size, docs_hbm, q_hbm, k_hbm, v_hbm, weights_ref, pen_ref, q_ref, kv_ref, docs_ref, sems):
    rest = [
        pltpu.make_async_copy(k_hbm, kv_ref.at[:BLK], sems.at[groups]),
        pltpu.make_async_copy(v_hbm, kv_ref.at[BLK:], sems.at[groups + 1]),
        pltpu.make_async_copy(docs_hbm, docs_ref, sems.at[groups + 2]),
    ]
    copies = []
    for g in range(groups):
        at = cut(g, size * HD)
        copies.append(pltpu.make_async_copy(q_hbm.at[:, at], q_ref.at[:, at], sems.at[g]))
    for copy in rest[:1] + copies + rest[1:]:
        copy.start()
    pen = jnp.concatenate([causal_pen()] * OWN_UNIT, axis=0)
    rest[0].wait()
    for unit in units_of(groups, size, OWN_UNIT):
        g, rows = unit[0], unit_rows(unit)
        if unit[1] == 0:
            copies[g].wait()
        weights_ref[g, rows] = weigh(dot_nt(unit_queries(q_ref, size, unit), kv_ref[:BLK, cut(g)]), pen)
    for copy in rest[1:]:
        copy.wait()
    for i, distance in enumerate((1, 2, 3)):
        pen_ref[i] = jnp.full((8, HD), penalty(docs_ref, lax.axis_index("ctx"), distance), F32)


def weigh_all(groups, size, q_ref, pen, k_ref, weights_ref):
    for unit in units_of(groups, size, ADD_UNIT):
        scores = dot_nt(unit_queries(q_ref, size, unit), k_ref[:BLK, cut(unit[0])])
        weights_ref[unit[0], unit_rows(unit)] = weigh(scores, pen)


def weights_kernel(groups, size, distances, q_ref, pen_ref, k_ref, weights_ref):
    position = lax.axis_index("ctx")
    even, odd = (pen_ref[d - 1][:1] for d in distances)

    @pl.when(position > 1)
    def _():
        weigh_all(groups, size, q_ref, jnp.where(lax.rem(position, 2) == 1, odd, even), k_ref, weights_ref)


def add_values(unit, weights, values):
    g, rows = unit[0], unit_rows(unit)
    left = jnp.concatenate([w[g, rows] for w in weights], axis=1)
    right = jnp.concatenate([v(g) for v in values], axis=0)
    return dot_nn(left, with_ones(right))


def part(ref, first=0):
    return lambda g: ref[first : first + BLK, cut(g)]


def finish(size, unit, both, result_ref, low_high):
    total = both[:, HD:]
    result = (both[:, :HD] / total).astype(BF16)
    g, first, count = unit
    for h in range(count):
        result_ref[:, cut(g * size + first + h)] = result[cut(h, BLK)]
        if low_high[0] is not None:
            low_high[0] = jnp.minimum(low_high[0], total[cut(h, BLK)])
        low_high[1] = jnp.maximum(low_high[1], total[cut(h, BLK)])


def new_range():
    return [jnp.ones((BLK, HD), F32)] * 2


def note_range(low_high, range_ref):
    if low_high[0] is not None:
        range_ref[0] = jnp.full((8, HD), jnp.min(low_high[0]), F32)
    range_ref[1] = jnp.full((8, HD), jnp.max(low_high[1]), F32)


def early_kernel(
    groups, size, q_ref, pen_ref, own_ref, kv_ref, a_ref, beside_k, beside_v, wa_ref, weights_ref, out_hbm, range_ref,
    result_ref, sem,
):
    position = lax.axis_index("ctx")
    range_ref[...] = jnp.ones_like(range_ref)

    @pl.when(position > 1)
    def _():
        weigh_all(groups, size, q_ref, pen_ref[1][:1], a_ref, wa_ref)

    @pl.when(lax.rem(position, 2) == 1)
    def _():
        weigh_all(groups, size, q_ref, pen_ref[0][:1], beside_k, weights_ref)

    def store_all(weights, values):
        low_high = new_range()
        for unit in units_of(groups, size, size):
            finish(size, unit, add_values(unit, weights, values), result_ref, low_high)
        note_range(low_high, range_ref)
        copy = pltpu.make_async_copy(result_ref, out_hbm, sem)
        copy.start()
        copy.wait()

    @pl.when(position == 0)
    def _():
        store_all([own_ref], [part(kv_ref, BLK)])

    @pl.when(position == 1)
    def _():
        store_all([own_ref, weights_ref], [part(kv_ref, BLK), part(beside_v)])


def values_kernel(
    groups, size, own_ref, wa_ref, wb_ref, ws_ref, kv_ref, va_ref, vb_ref, vs_ref, early_range, both_ref, range_ref,
):
    position = lax.axis_index("ctx")
    odd = lax.rem(position, 2) == 1
    range_ref[...] = early_range[...]

    def whole(weights, values):
        low = jnp.ones((BLK, HD), F32)
        for unit in units_of(groups, size, ADD_UNIT):
            both = add_values(unit, weights, values)
            both_ref[unit[0], unit_rows(unit)] = both
            for h in range(unit[2]):
                low = jnp.minimum(low, both[cut(h, BLK), HD:])
        range_ref[0] = jnp.full((8, HD), jnp.min(low), F32)

    weights = [own_ref, wa_ref, wb_ref]
    values = [part(kv_ref, BLK), part(va_ref), part(vb_ref)]

    @pl.when(jnp.logical_not(odd) & (position > 1))
    def _():
        whole(weights, values)

    @pl.when(odd & (position > 1))
    def _():
        whole(weights + [ws_ref], values + [part(vs_ref)])


def last_kernel(
    groups, size, q_ref, pen_ref, both_ref, c_ref, own_ref, wa_ref, wb_ref, ws_ref, kv_ref, ak_ref, av_ref, bk_ref, bv_ref, sk_ref, sv_ref, early_range, _, out_hbm, result_ref, range_ref, sems,
):
    position = lax.axis_index("ctx")
    odd = lax.rem(position, 2) == 1
    units = units_of(groups, size, LAST_UNIT)
    copies = {}
    for n, unit in enumerate(units):
        start = (unit[0] * size + unit[1]) * HD
        at = slice(start, start + unit[2] * HD)
        copies[unit] = pltpu.make_async_copy(result_ref.at[:, at], out_hbm.at[:, at], sems.at[n])
    range_ref[...] = early_range[...]

    @pl.when(jnp.logical_not(odd) & (position > 1))
    def _():
        low_high = [None, new_range()[1]]
        pen = pen_ref[2][:1]

        def first(unit):
            return weigh(dot_nt(unit_queries(q_ref, size, unit), c_ref[:BLK, cut(unit[0])]), pen)

        def second(unit, weights):
            values = with_ones(c_ref[BLK:, cut(unit[0])])
            both = both_ref[unit[0], unit_rows(unit)] + dot_nn(weights, values)
            finish(size, unit, both, result_ref, low_high)
            copies[unit].start()

        staggered(units, first, second)
        note_range(low_high, range_ref)

    @pl.when(odd & (position > 1))
    def _():
        low_high = [None, new_range()[1]]
        for unit in units:
            finish(size, unit, both_ref[unit[0], unit_rows(unit)], result_ref, low_high)
            copies[unit].start()
        note_range(low_high, range_ref)

    safe = (jnp.min(range_ref[0]) > LOW) & (jnp.max(range_ref[1]) < HIGH)

    @pl.when(position > 1)
    def _():
        for copy in copies.values():
            copy.wait()

    @pl.when(jnp.logical_not(safe))
    def _():
        pens = [causal_pen()] + [pen_ref[i][:1] for i in range(3)]
        pairs = (((bk_ref, bv_ref, 0), (sk_ref, sv_ref, 0)), ((ak_ref, av_ref, 0),) * 2, ((c_ref, c_ref, BLK), (bk_ref, bv_ref, 0)))
        for g in range(groups):
            keys = [kv_ref[:BLK, cut(g)]]
            values = [kv_ref[BLK:, cut(g)]]
            for (ek, ev, first), (ok, ov, _) in pairs:
                keys.append(jnp.where(odd, ok[:BLK, cut(g)], ek[:BLK, cut(g)]))
                values.append(jnp.where(odd, ov[:BLK, cut(g)], ev[first : first + BLK, cut(g)]))

            def one_head(h, _):
                at = pl.ds(pl.multiple_of((g * size + h) * HD, HD), HD)
                queries = q_ref[:, at]
                scores = [dot_nt(queries, x) - pen for x, pen in zip(keys, pens)]
                top = functools.reduce(jnp.maximum, [jnp.max(x, axis=1, keepdims=True) for x in scores])
                weights = [jnp.exp2((x - top) * EXP2_SCALE) for x in scores]
                total = sum(jnp.sum(w, axis=1, keepdims=True) for w in weights)
                product = sum(dot_nn(w.astype(BF16), x) for w, x in zip(weights, values))
                result_ref[:, at] = (product / total).astype(BF16)
                return 0

            lax.fori_loop(0, size, one_head, 0)
        store = pltpu.make_async_copy(result_ref, out_hbm, sems.at[0])
        store.start()
        store.wait()


def routes(n):
    step = n // 4
    ring = [(i, (i + 2) % n) for i in range(n)]
    across = {i: i + 3 for i in range(1, n - 3, 2)}
    first = [n - 3 - step * k for k in (1, 2, 3)] + [2]
    second = [n - 5 - step * k for k in (0, 1, 2)] + [step + 1, 0]
    for at, places in ((n - 3, first), (n - 1, second)):
        for place in places:
            across[at] = place
            at = place - 1
    across.update({i: i + 1 for i in range(0, n, 2) if i not in across})
    swap = [(i, i ^ 1) for i in range(n)]
    return ring, sorted(across.items()), swap


def in_hbm(array):
    return pltpu.with_memory_space_constraint(array, pltpu.HBM)


def after(value, *others):
    return lax.optimization_barrier((value, *others))[0]


def on_device(queries, keys, values, docs):
    row_count, width = keys.shape
    groups = width // HD
    size = queries.shape[1] // width
    rows = size * BLK
    n = lax.axis_size("ctx")
    assert row_count == BLK and n % 16 == 0
    ring, across, swap = routes(n)
    cost = pl.CostEstimate(flops=0, bytes_accessed=0, transcendentals=0)
    weights_shape = jax.ShapeDtypeStruct((groups, rows, HD), BF16)
    both_shape = jax.ShapeDtypeStruct((groups, rows, 2 * HD), F32)
    pack_shape = jax.ShapeDtypeStruct((2 * BLK, width), BF16)
    range_shape = jax.ShapeDtypeStruct((2, 8, HD), F32)
    result = jax.ShapeDtypeStruct(queries.shape, BF16)
    dma = pltpu.SemaphoreType.DMA

    def call(kernel, name, out_shape, operands, out_specs=None, in_specs=None, scratch_shapes=(), **options):
        many = isinstance(out_shape, tuple)
        return pl.pallas_call(
            kernel,
            out_shape=out_shape,
            in_specs=in_specs or [VMEM] * len(operands),
            out_specs=out_specs or ((VMEM,) * len(out_shape) if many else VMEM),
            scratch_shapes=scratch_shapes,
            compiler_params=PARAMS,
            cost_estimate=cost,
            name=name,
            **options,
        )(*operands)

    def move(block, route):
        return lax.ppermute(block, "ctx", route)

    def own():
        return call(
            functools.partial(own_kernel, groups, size), "own_block",
            (weights_shape, jax.ShapeDtypeStruct((3, 8, HD), F32), result, pack_shape),
            [in_hbm(x) for x in (docs, queries, keys, values)], in_specs=[HBM] * 4,
            scratch_shapes=[pltpu.SMEM(docs.shape, jnp.int32), dma((groups + 3,))],
        )

    def early(*operands):
        return call(
            functools.partial(early_kernel, groups, size), "early_rows",
            (weights_shape, weights_shape, result, range_shape), operands, out_specs=(VMEM, VMEM, HBM, VMEM),
            scratch_shapes=[pltpu.VMEM(result.shape, BF16), dma(())],
        )

    def weigh_block(name, distances, *operands):
        return call(functools.partial(weights_kernel, groups, size, distances), name, weights_shape, operands)

    ak, av = move(keys, ring), move(values, ring)
    sk, sv = move(keys, swap), move(values, swap)
    w_own, pen, local, block = own()
    block_c = move(after(block, pen), across)
    w_a, w_s, stored, early_range = early(local, pen, w_own, block, ak, sk, sv)
    bk = move(after(ak, pen), swap)
    bv = move(after(av, w_a), swap)
    w_b = weigh_block("third_weights", (1, 3), local, pen, bk)
    both, early_range = call(
        functools.partial(values_kernel, groups, size), "values", (both_shape, range_shape),
        (w_own, w_a, w_b, w_s, block, av, bv, sv, early_range),
    )
    operands = (local, pen, both, block_c, w_own, w_a, w_b, w_s, block, ak, av, bk, bv, sk, sv, early_range, in_hbm(stored))
    return call(
        functools.partial(last_kernel, groups, size), "last_blocks", result, operands,
        in_specs=[VMEM] * 16 + [HBM], out_specs=HBM, input_output_aliases={16: 0},
        scratch_shapes=[pltpu.VMEM(result.shape, BF16), pltpu.VMEM(range_shape.shape, F32), dma((groups * size // LAST_UNIT,))],
    )


def solution(mesh):
    return jax.shard_map(
        on_device,
        mesh=mesh,
        in_specs=(
            P(("seq", "ctx"), None),
            P(("seq", "ctx"), None),
            P(("seq", "ctx"), None),
            P("seq"),
        ),
        out_specs=P(("seq", "ctx"), None),
        check_vma=False,
    )
```

```python
import functools
import math

import jax
import jax.numpy as jnp
from jax import lax
from jax.experimental import pallas as pl
from jax.experimental.pallas import tpu as pltpu
from jax.sharding import PartitionSpec as P

HD = 128
BLK = 128
NEG = -1e30
LOW, HIGH = 1e-25, 1e35
EXP2_SCALE = math.log2(math.e) / math.sqrt(HD)
OWN_UNIT, ADD_UNIT, LAST_UNIT = 4, 8, 8
F32 = jnp.float32
BF16 = jnp.bfloat16
VMEM = pl.BlockSpec(memory_space=pltpu.VMEM)
HBM = pl.BlockSpec(memory_space=pltpu.HBM)
PARAMS = pltpu.CompilerParams(vmem_limit_bytes=40 * 1024 * 1024)


def dot_nt(a, b):
    return lax.dot_general(a, b, (((1,), (1,)), ((), ())), preferred_element_type=F32)


def dot_nn(a, b):
    return lax.dot_general(a, b, (((1,), (0,)), ((), ())), preferred_element_type=F32)


def cut(index, width=HD):
    return slice(index * width, (index + 1) * width)


def with_ones(values):
    return jnp.concatenate([values, jnp.ones_like(values)], axis=1)


def unit_queries(q_ref, size, unit):
    g, first, count = unit
    return jnp.concatenate([q_ref[:, cut(g * size + first + h)] for h in range(count)], axis=0)


def unit_rows(unit):
    return slice(unit[1] * BLK, (unit[1] + unit[2]) * BLK)


def units_of(groups, size, count):
    return [(g, first, count) for g in range(groups) for first in range(0, size, count)]


def staggered(units, first, second):
    waiting = None
    for unit in units:
        ready = (unit, first(unit))
        if waiting is not None:
            second(*waiting)
        waiting = ready
    second(*waiting)


def penalty(docs_ref, position, distance):
    source = position - distance
    same = docs_ref[jnp.maximum(source, 0)] == docs_ref[position]
    return jnp.where((source >= 0) & same, 0.0, -NEG).astype(F32)


def weigh(scores, pen):
    return jnp.exp2(scores * EXP2_SCALE - pen).astype(BF16)


def causal_pen():
    row = lax.broadcasted_iota(jnp.int32, (BLK, BLK), 0)
    col = lax.broadcasted_iota(jnp.int32, (BLK, BLK), 1)
    return jnp.where(col <= row, 0.0, -NEG).astype(F32)


def own_kernel(groups, size, docs_hbm, q_hbm, k_hbm, v_hbm, weights_ref, pen_ref, q_ref, kv_ref, docs_ref, sems):
    rest = [
        pltpu.make_async_copy(k_hbm, kv_ref.at[:BLK], sems.at[groups]),
        pltpu.make_async_copy(v_hbm, kv_ref.at[BLK:], sems.at[groups + 1]),
        pltpu.make_async_copy(docs_hbm, docs_ref, sems.at[groups + 2]),
    ]
    copies = []
    for g in range(groups):
        at = cut(g, size * HD)
        copies.append(pltpu.make_async_copy(q_hbm.at[:, at], q_ref.at[:, at], sems.at[g]))
    for copy in rest[:1] + copies + rest[1:]:
        copy.start()
    pen = jnp.concatenate([causal_pen()] * OWN_UNIT, axis=0)
    rest[0].wait()
    for unit in units_of(groups, size, OWN_UNIT):
        g, rows = unit[0], unit_rows(unit)
        if unit[1] == 0:
            copies[g].wait()
        weights_ref[g, rows] = weigh(dot_nt(unit_queries(q_ref, size, unit), kv_ref[:BLK, cut(g)]), pen)
    for copy in rest[1:]:
        copy.wait()
    for i, distance in enumerate((1, 2, 3)):
        pen_ref[i] = jnp.full((8, HD), penalty(docs_ref, lax.axis_index("ctx"), distance), F32)


def weigh_all(groups, size, q_ref, pen, k_ref, weights_ref):
    for unit in units_of(groups, size, ADD_UNIT):
        scores = dot_nt(unit_queries(q_ref, size, unit), k_ref[:BLK, cut(unit[0])])
        weights_ref[unit[0], unit_rows(unit)] = weigh(scores, pen)


def weights_kernel(groups, size, distances, q_ref, pen_ref, k_ref, rows_ref, weights_ref, out_hbm, sem):
    position = lax.axis_index("ctx")
    even, odd = (pen_ref[d - 1][:1] for d in distances)

    @pl.when(position > 1)
    def _():
        weigh_all(groups, size, q_ref, jnp.where(lax.rem(position, 2) == 1, odd, even), k_ref, weights_ref)

    @pl.when(position <= 1)
    def _():
        copy = pltpu.make_async_copy(rows_ref, out_hbm, sem)
        copy.start()
        copy.wait()


def add_values(unit, weights, values):
    g, rows = unit[0], unit_rows(unit)
    left = jnp.concatenate([w[g, rows] for w in weights], axis=1)
    right = jnp.concatenate([v(g) for v in values], axis=0)
    return dot_nn(left, with_ones(right))


def part(ref, first=0):
    return lambda g: ref[first : first + BLK, cut(g)]


def finish(size, unit, both, result_ref, low_high):
    total = both[:, HD:]
    result = (both[:, :HD] / total).astype(BF16)
    g, first, count = unit
    for h in range(count):
        result_ref[:, cut(g * size + first + h)] = result[cut(h, BLK)]
        if low_high[0] is not None:
            low_high[0] = jnp.minimum(low_high[0], total[cut(h, BLK)])
        low_high[1] = jnp.maximum(low_high[1], total[cut(h, BLK)])


def new_range():
    return [jnp.ones((BLK, HD), F32)] * 2


def note_range(low_high, range_ref):
    if low_high[0] is not None:
        range_ref[0] = jnp.full((8, HD), jnp.min(low_high[0]), F32)
    range_ref[1] = jnp.full((8, HD), jnp.max(low_high[1]), F32)


def early_kernel(
    groups, size, q_ref, pen_ref, own_ref, kv_ref, a_ref, beside_k, beside_v, wa_ref, weights_ref, result_ref, range_ref,
):
    position = lax.axis_index("ctx")
    range_ref[...] = jnp.ones_like(range_ref)

    @pl.when(position > 1)
    def _():
        weigh_all(groups, size, q_ref, pen_ref[1][:1], a_ref, wa_ref)

    @pl.when(lax.rem(position, 2) == 1)
    def _():
        weigh_all(groups, size, q_ref, pen_ref[0][:1], beside_k, weights_ref)

    def store_all(weights, values):
        low_high = new_range()
        for unit in units_of(groups, size, size):
            finish(size, unit, add_values(unit, weights, values), result_ref, low_high)
        note_range(low_high, range_ref)

    @pl.when(position == 0)
    def _():
        store_all([own_ref], [part(kv_ref, BLK)])

    @pl.when(position == 1)
    def _():
        store_all([own_ref, weights_ref], [part(kv_ref, BLK), part(beside_v)])


def values_kernel(
    groups, size, own_ref, wa_ref, ws_ref, kv_ref, va_ref, vs_ref, early_range, both_ref, range_ref,
):
    position = lax.axis_index("ctx")
    odd = lax.rem(position, 2) == 1
    range_ref[...] = early_range[...]

    def whole(weights, values):
        low = jnp.ones((BLK, HD), F32)
        for unit in units_of(groups, size, ADD_UNIT):
            both = add_values(unit, weights, values)
            both_ref[unit[0], unit_rows(unit)] = both
            for h in range(unit[2]):
                low = jnp.minimum(low, both[cut(h, BLK), HD:])
        range_ref[0] = jnp.full((8, HD), jnp.min(low), F32)

    weights = [own_ref, wa_ref]
    values = [part(kv_ref, BLK), part(va_ref)]

    @pl.when(jnp.logical_not(odd) & (position > 1))
    def _():
        whole(weights, values)

    @pl.when(odd & (position > 1))
    def _():
        whole(weights + [ws_ref], values + [part(vs_ref)])


def out_copies(units, size, result_ref, out_hbm, sems):
    copies = {}
    for n, unit in enumerate(units):
        start = (unit[0] * size + unit[1]) * HD
        at = slice(start, start + unit[2] * HD)
        copies[unit] = pltpu.make_async_copy(result_ref.at[:, at], out_hbm.at[:, at], sems.at[n])
    return copies


def odd_kernel(groups, size, both_ref, wb_ref, bv_ref, so_far, _, out_hbm, range_ref, result_ref, sems):
    position = lax.axis_index("ctx")
    range_ref[...] = so_far[...]

    @pl.when((lax.rem(position, 2) == 1) & (position > 1))
    def _():
        units = units_of(groups, size, LAST_UNIT)
        copies = out_copies(units, size, result_ref, out_hbm, sems)
        low_high = [None, new_range()[1]]
        for unit in units:
            both = both_ref[unit[0], unit_rows(unit)] + add_values(unit, [wb_ref], [part(bv_ref)])
            finish(size, unit, both, result_ref, low_high)
            copies[unit].start()
        note_range(low_high, range_ref)
        for copy in copies.values():
            copy.wait()


def last_kernel(
    groups, size, q_ref, pen_ref, both_ref, c_ref, own_ref, wa_ref, wb_ref, ws_ref, kv_ref,
    ak_ref, av_ref, bk_ref, bv_ref, sk_ref, sv_ref, so_far, _, out_hbm, result_ref, range_ref, sems,
):
    position = lax.axis_index("ctx")
    odd = lax.rem(position, 2) == 1
    units = units_of(groups, size, LAST_UNIT)
    copies = out_copies(units, size, result_ref, out_hbm, sems)
    range_ref[...] = so_far[...]
    waits = jnp.logical_not(odd) & (position > 1)

    @pl.when(waits)
    def _():
        low_high = [None, new_range()[1]]
        pen = pen_ref[2][:1]

        def first(unit):
            return weigh(dot_nt(unit_queries(q_ref, size, unit), c_ref[:BLK, cut(unit[0])]), pen)

        def second(unit, weights):
            g, at = unit[0], unit_rows(unit)
            weights = jnp.concatenate([wb_ref[g, at], weights], axis=1)
            values = jnp.concatenate([bv_ref[:, cut(g)], c_ref[BLK:, cut(g)]], axis=0)
            both = both_ref[g, at] + dot_nn(weights, with_ones(values))
            finish(size, unit, both, result_ref, low_high)
            copies[unit].start()

        staggered(units, first, second)
        note_range(low_high, range_ref)

    safe = (jnp.min(range_ref[0]) > LOW) & (jnp.max(range_ref[1]) < HIGH)

    @pl.when(waits)
    def _():
        for copy in copies.values():
            copy.wait()

    @pl.when(jnp.logical_not(safe))
    def _():
        pens = [causal_pen()] + [pen_ref[i][:1] for i in range(3)]
        pairs = (((bk_ref, bv_ref, 0), (sk_ref, sv_ref, 0)), ((ak_ref, av_ref, 0),) * 2, ((c_ref, c_ref, BLK), (bk_ref, bv_ref, 0)))
        for g in range(groups):
            keys = [kv_ref[:BLK, cut(g)]]
            values = [kv_ref[BLK:, cut(g)]]
            for (ek, ev, first), (ok, ov, _) in pairs:
                keys.append(jnp.where(odd, ok[:BLK, cut(g)], ek[:BLK, cut(g)]))
                values.append(jnp.where(odd, ov[:BLK, cut(g)], ev[first : first + BLK, cut(g)]))

            def one_head(h, _):
                at = pl.ds(pl.multiple_of((g * size + h) * HD, HD), HD)
                queries = q_ref[:, at]
                scores = [dot_nt(queries, x) - pen for x, pen in zip(keys, pens)]
                top = functools.reduce(jnp.maximum, [jnp.max(x, axis=1, keepdims=True) for x in scores])
                weights = [jnp.exp2((x - top) * EXP2_SCALE) for x in scores]
                total = sum(jnp.sum(w, axis=1, keepdims=True) for w in weights)
                product = sum(dot_nn(w.astype(BF16), x) for w, x in zip(weights, values))
                result_ref[:, at] = (product / total).astype(BF16)
                return 0

            lax.fori_loop(0, size, one_head, 0)
        store = pltpu.make_async_copy(result_ref, out_hbm, sems.at[0])
        store.start()
        store.wait()


def routes(n):
    step = n // 4
    ring = [(i, (i + 2) % n) for i in range(n)]
    across = {i: i + 3 for i in range(1, n - 3, 2)}
    first = [n - 3 - step * k for k in (1, 2, 3)] + [2]
    second = [n - 5 - step * k for k in (0, 1, 2)] + [step + 1, 0]
    for at, places in ((n - 3, first), (n - 1, second)):
        for place in places:
            across[at] = place
            at = place - 1
    across.update({i: i + 1 for i in range(0, n, 2) if i not in across})
    swap = [(i, i ^ 1) for i in range(n)]
    return ring, sorted(across.items()), swap


def in_hbm(array):
    return pltpu.with_memory_space_constraint(array, pltpu.HBM)


def after(value, *others):
    return lax.optimization_barrier((value, *others))[0]


def on_device(queries, keys, values, docs):
    row_count, width = keys.shape
    groups = width // HD
    size = queries.shape[1] // width
    rows = size * BLK
    n = lax.axis_size("ctx")
    assert row_count == BLK and n % 16 == 0
    ring, across, swap = routes(n)
    cost = pl.CostEstimate(flops=0, bytes_accessed=0, transcendentals=0)
    weights_shape = jax.ShapeDtypeStruct((groups, rows, HD), BF16)
    both_shape = jax.ShapeDtypeStruct((groups, rows, 2 * HD), F32)
    pack_shape = jax.ShapeDtypeStruct((2 * BLK, width), BF16)
    range_shape = jax.ShapeDtypeStruct((2, 8, HD), F32)
    result = jax.ShapeDtypeStruct(queries.shape, BF16)
    dma = pltpu.SemaphoreType.DMA

    def call(kernel, name, out_shape, operands, out_specs=None, in_specs=None, scratch_shapes=(), **options):
        many = isinstance(out_shape, tuple)
        return pl.pallas_call(
            kernel,
            out_shape=out_shape,
            in_specs=in_specs or [VMEM] * len(operands),
            out_specs=out_specs or ((VMEM,) * len(out_shape) if many else VMEM),
            scratch_shapes=scratch_shapes,
            compiler_params=PARAMS,
            cost_estimate=cost,
            name=name,
            **options,
        )(*operands)

    def move(block, route):
        return lax.ppermute(block, "ctx", route)

    def own():
        return call(
            functools.partial(own_kernel, groups, size), "own_block",
            (weights_shape, jax.ShapeDtypeStruct((3, 8, HD), F32), result, pack_shape),
            [in_hbm(x) for x in (docs, queries, keys, values)], in_specs=[HBM] * 4,
            scratch_shapes=[pltpu.SMEM(docs.shape, jnp.int32), dma((groups + 3,))],
        )

    def early(*operands):
        return call(
            functools.partial(early_kernel, groups, size), "early_rows",
            (weights_shape, weights_shape, result, range_shape), operands,
        )

    def weigh_block(name, distances, *operands):
        return call(
            functools.partial(weights_kernel, groups, size, distances), name, (weights_shape, result), operands,
            out_specs=(VMEM, HBM), scratch_shapes=[dma(())],
        )

    ak, av = move(keys, ring), move(values, ring)
    sk, sv = move(keys, swap), move(values, swap)
    w_own, pen, local, block = own()
    block_c = move(after(block, pen), across)
    w_a, w_s, first_rows, early_range = early(local, pen, w_own, block, ak, sk, sv)
    bk = move(after(ak, pen), swap)
    bv = move(after(av, w_a), swap)
    w_b, stored = weigh_block("third_weights", (1, 3), local, pen, bk, first_rows)
    both, early_range = call(
        functools.partial(values_kernel, groups, size), "values", (both_shape, range_shape),
        (w_own, w_a, w_s, block, av, sv, early_range),
    )
    unit_sems = dma((groups * size // LAST_UNIT,))
    stored, so_far = call(
        functools.partial(odd_kernel, groups, size), "odd_rows", (result, range_shape), (both, w_b, bv, early_range, in_hbm(stored)),
        in_specs=[VMEM] * 4 + [HBM], out_specs=(HBM, VMEM), input_output_aliases={4: 0},
        scratch_shapes=[pltpu.VMEM(result.shape, BF16), unit_sems],
    )
    operands = (local, pen, both, block_c, w_own, w_a, w_b, w_s, block, ak, av, bk, bv, sk, sv, so_far, in_hbm(stored))
    return call(
        functools.partial(last_kernel, groups, size), "last_blocks", result, operands,
        in_specs=[VMEM] * 16 + [HBM], out_specs=HBM, input_output_aliases={16: 0},
        scratch_shapes=[pltpu.VMEM(result.shape, BF16), pltpu.VMEM(range_shape.shape, F32), unit_sems],
    )


def solution(mesh):
    return jax.shard_map(
        on_device,
        mesh=mesh,
        in_specs=(
            P(("seq", "ctx"), None),
            P(("seq", "ctx"), None),
            P(("seq", "ctx"), None),
            P("seq"),
        ),
        out_specs=P(("seq", "ctx"), None),
        check_vma=False,
    )
```

```python
import functools
import math

import jax
import jax.numpy as jnp
from jax import lax
from jax.experimental import pallas as pl
from jax.experimental.pallas import tpu as pltpu
from jax.sharding import PartitionSpec as P

HD = 128
BLK = 128
NEG = -1e30
LOW, HIGH = 1e-25, 1e35
EXP2_SCALE = math.log2(math.e) / math.sqrt(HD)
OWN_UNIT, ADD_UNIT, LAST_UNIT = 4, 8, 8
F32 = jnp.float32
BF16 = jnp.bfloat16
VMEM = pl.BlockSpec(memory_space=pltpu.VMEM)
HBM = pl.BlockSpec(memory_space=pltpu.HBM)
PARAMS = pltpu.CompilerParams(vmem_limit_bytes=40 * 1024 * 1024)


def dot_nt(a, b):
    return lax.dot_general(a, b, (((1,), (1,)), ((), ())), preferred_element_type=F32)


def dot_nn(a, b):
    return lax.dot_general(a, b, (((1,), (0,)), ((), ())), preferred_element_type=F32)


def cut(index, width=HD):
    return slice(index * width, (index + 1) * width)


def with_ones(values):
    return jnp.concatenate([values, jnp.ones_like(values)], axis=1)


def unit_queries(q_ref, size, unit):
    g, first, count = unit
    return jnp.concatenate([q_ref[:, cut(g * size + first + h)] for h in range(count)], axis=0)


def unit_rows(unit):
    return slice(unit[1] * BLK, (unit[1] + unit[2]) * BLK)


def units_of(groups, size, count):
    return [(g, first, count) for g in range(groups) for first in range(0, size, count)]


def staggered(units, first, second):
    waiting = None
    for unit in units:
        ready = (unit, first(unit))
        if waiting is not None:
            second(*waiting)
        waiting = ready
    second(*waiting)


def penalty(docs_ref, position, distance):
    source = position - distance
    same = docs_ref[jnp.maximum(source, 0)] == docs_ref[position]
    return jnp.where((source >= 0) & same, 0.0, -NEG).astype(F32)


def weigh(scores, pen):
    return jnp.exp2(scores * EXP2_SCALE - pen).astype(BF16)


def causal_pen():
    row = lax.broadcasted_iota(jnp.int32, (BLK, BLK), 0)
    col = lax.broadcasted_iota(jnp.int32, (BLK, BLK), 1)
    return jnp.where(col <= row, 0.0, -NEG).astype(F32)


def own_kernel(groups, size, docs_hbm, q_hbm, k_hbm, v_hbm, weights_ref, pen_ref, q_ref, kv_ref, docs_ref, sems):
    rest = [
        pltpu.make_async_copy(k_hbm, kv_ref.at[:BLK], sems.at[groups]),
        pltpu.make_async_copy(v_hbm, kv_ref.at[BLK:], sems.at[groups + 1]),
        pltpu.make_async_copy(docs_hbm, docs_ref, sems.at[groups + 2]),
    ]
    copies = []
    for g in range(groups):
        at = cut(g, size * HD)
        copies.append(pltpu.make_async_copy(q_hbm.at[:, at], q_ref.at[:, at], sems.at[g]))
    for copy in rest[:1] + copies + rest[1:]:
        copy.start()
    pen = jnp.concatenate([causal_pen()] * OWN_UNIT, axis=0)
    rest[0].wait()
    for unit in units_of(groups, size, OWN_UNIT):
        g, rows = unit[0], unit_rows(unit)
        if unit[1] == 0:
            copies[g].wait()
        weights_ref[g, rows] = weigh(dot_nt(unit_queries(q_ref, size, unit), kv_ref[:BLK, cut(g)]), pen)
    for copy in rest[1:]:
        copy.wait()
    for i, distance in enumerate((1, 2, 3)):
        pen_ref[i] = jnp.full((8, HD), penalty(docs_ref, lax.axis_index("ctx"), distance), F32)


def weigh_all(groups, size, q_ref, pen, k_ref, weights_ref):
    for unit in units_of(groups, size, ADD_UNIT):
        scores = dot_nt(unit_queries(q_ref, size, unit), k_ref[:BLK, cut(unit[0])])
        weights_ref[unit[0], unit_rows(unit)] = weigh(scores, pen)


def weights_kernel(groups, size, distances, q_ref, pen_ref, k_ref, kv_ref, sk_ref, sv_ref, so_far, rows_ref, _, weights_ref, out_hbm, result_ref, sem):
    position = lax.axis_index("ctx")
    even, odd = (pen_ref[d - 1][:1] for d in distances)

    @pl.when(position > 1)
    def _():
        weigh_all(groups, size, q_ref, jnp.where(lax.rem(position, 2) == 1, odd, even), k_ref, weights_ref)

    @pl.when(position == 1)
    def _():
        copy = pltpu.make_async_copy(rows_ref, out_hbm, sem)
        copy.start()
        copy.wait()

    @pl.when((position <= 1) & jnp.logical_not(is_safe(so_far)))
    def _():
        def blocks(g):
            yield kv_ref[:BLK, cut(g)], kv_ref[BLK:, cut(g)]
            yield sk_ref[:, cut(g)], sv_ref[:, cut(g)]

        exact_rows(groups, size, q_ref, blocks, [causal_pen(), pen_ref[0][:1]], result_ref, out_hbm, sem)


def add_values(unit, weights, values):
    g, rows = unit[0], unit_rows(unit)
    left = jnp.concatenate([w[g, rows] for w in weights], axis=1)
    right = jnp.concatenate([v(g) for v in values], axis=0)
    return dot_nn(left, with_ones(right))


def part(ref, first=0):
    return lambda g: ref[first : first + BLK, cut(g)]


def finish(size, unit, both, result_ref, low_high):
    total = both[:, HD:]
    result = (both[:, :HD] / total).astype(BF16)
    g, first, count = unit
    for h in range(count):
        result_ref[:, cut(g * size + first + h)] = result[cut(h, BLK)]
        if low_high[0] is not None:
            low_high[0] = jnp.minimum(low_high[0], total[cut(h, BLK)])
        low_high[1] = jnp.maximum(low_high[1], total[cut(h, BLK)])


def new_range():
    return [jnp.ones((BLK, HD), F32)] * 2


def note_range(low_high, range_ref):
    if low_high[0] is not None:
        range_ref[0] = jnp.full((8, HD), jnp.min(low_high[0]), F32)
    range_ref[1] = jnp.full((8, HD), jnp.max(low_high[1]), F32)


def is_safe(range_ref):
    in_range = (range_ref[0] > LOW) & (range_ref[1] < HIGH)
    return jnp.min(jnp.where(in_range, 1.0, 0.0)) > 0.5


def exact_rows(groups, size, q_ref, blocks, pens, result_ref, out_hbm, sem):
    for g in range(groups):
        keys, values = zip(*blocks(g))

        def one_head(h, _):
            at = pl.ds(pl.multiple_of((g * size + h) * HD, HD), HD)
            queries = q_ref[:, at]
            scores = [dot_nt(queries, x) - pen for x, pen in zip(keys, pens)]
            top = functools.reduce(jnp.maximum, [jnp.max(x, axis=1, keepdims=True) for x in scores])
            weights = [jnp.exp2((x - top) * EXP2_SCALE) for x in scores]
            total = sum(jnp.sum(w, axis=1, keepdims=True) for w in weights)
            product = sum(dot_nn(w.astype(BF16), x) for w, x in zip(weights, values))
            result_ref[:, at] = (product / total).astype(BF16)
            return 0

        lax.fori_loop(0, size, one_head, 0)
    store = pltpu.make_async_copy(result_ref, out_hbm, sem)
    store.start()
    store.wait()


def early_kernel(
    groups, size, q_ref, pen_ref, own_ref, kv_ref, a_ref, beside_k, beside_v, wa_ref, weights_ref, result_ref, out_hbm, range_ref, sem,
):
    position = lax.axis_index("ctx")
    range_ref[...] = jnp.ones_like(range_ref)

    @pl.when(position > 1)
    def _():
        weigh_all(groups, size, q_ref, pen_ref[1][:1], a_ref, wa_ref)

    @pl.when(lax.rem(position, 2) == 1)
    def _():
        weigh_all(groups, size, q_ref, pen_ref[0][:1], beside_k, weights_ref)

    def store_all(weights, values):
        low_high = new_range()
        for unit in units_of(groups, size, size):
            finish(size, unit, add_values(unit, weights, values), result_ref, low_high)
        note_range(low_high, range_ref)

    @pl.when(position == 0)
    def _():
        store_all([own_ref], [part(kv_ref, BLK)])
        copy = pltpu.make_async_copy(result_ref, out_hbm, sem)
        copy.start()
        copy.wait()

    @pl.when(position == 1)
    def _():
        store_all([own_ref, weights_ref], [part(kv_ref, BLK), part(beside_v)])


def values_kernel(groups, size, parity, own_ref, wa_ref, ws_ref, kv_ref, va_ref, vs_ref, so_far, *refs):
    both_ref, range_ref = refs[-2:]
    position = lax.axis_index("ctx")
    range_ref[...] = so_far[...]

    @pl.when((lax.rem(position, 2) == parity) & (position > 1))
    def _():
        weights = [own_ref, wa_ref] + [ws_ref] * parity
        values = [part(kv_ref, BLK), part(va_ref)] + [part(vs_ref)] * parity
        low = jnp.ones((BLK, HD), F32)
        for unit in units_of(groups, size, ADD_UNIT):
            both = add_values(unit, weights, values)
            both_ref[unit[0], unit_rows(unit)] = both
            for h in range(unit[2]):
                low = jnp.minimum(low, both[cut(h, BLK), HD:])
        range_ref[0] = jnp.full((8, HD), jnp.min(low), F32)


def out_copies(units, size, result_ref, out_hbm, sems):
    copies = {}
    for n, unit in enumerate(units):
        start = (unit[0] * size + unit[1]) * HD
        at = slice(start, start + unit[2] * HD)
        copies[unit] = pltpu.make_async_copy(result_ref.at[:, at], out_hbm.at[:, at], sems.at[n])
    return copies


def all_here(position):
    return (lax.rem(position, 2) == 1) | (position < 3)


def complete_kernel(groups, size, both_ref, wb_ref, bv_ref, so_far, _, out_hbm, range_ref, result_ref, sems):
    position = lax.axis_index("ctx")
    range_ref[...] = so_far[...]

    @pl.when(all_here(position) & (position > 1))
    def _():
        units = units_of(groups, size, LAST_UNIT)
        copies = out_copies(units, size, result_ref, out_hbm, sems)
        low_high = [None, new_range()[1]]
        for unit in units:
            both = both_ref[unit[0], unit_rows(unit)] + add_values(unit, [wb_ref], [part(bv_ref)])
            finish(size, unit, both, result_ref, low_high)
            copies[unit].start()
        note_range(low_high, range_ref)
        for copy in copies.values():
            copy.wait()


def last_kernel(
    groups, size, q_ref, pen_ref, both_ref, c_ref, own_ref, wa_ref, wb_ref, ws_ref, kv_ref,
    ak_ref, av_ref, bk_ref, bv_ref, sk_ref, sv_ref, so_far, _, out_hbm, result_ref, range_ref, safe_ref, sems,
):
    position = lax.axis_index("ctx")
    odd = lax.rem(position, 2) == 1
    units = units_of(groups, size, LAST_UNIT)
    copies = out_copies(units, size, result_ref, out_hbm, sems)
    range_ref[...] = so_far[...]
    waits = jnp.logical_not(all_here(position))
    safe_ref[0] = 1

    def check():
        safe_ref[0] = jnp.where(is_safe(range_ref), 1, 0)

    @pl.when(jnp.logical_not(waits) & (position > 1))
    def _():
        check()

    @pl.when(waits)
    def _():
        low_high = [None, new_range()[1]]
        pen = pen_ref[2][:1]

        def first(unit):
            return weigh(dot_nt(unit_queries(q_ref, size, unit), c_ref[:BLK, cut(unit[0])]), pen)

        def second(unit, weights):
            g, at = unit[0], unit_rows(unit)
            weights = jnp.concatenate([wb_ref[g, at], weights], axis=1)
            values = jnp.concatenate([bv_ref[:, cut(g)], c_ref[BLK:, cut(g)]], axis=0)
            both = both_ref[g, at] + dot_nn(weights, with_ones(values))
            finish(size, unit, both, result_ref, low_high)
            copies[unit].start()

        staggered(units, first, second)
        note_range(low_high, range_ref)
        check()
        for copy in copies.values():
            copy.wait()

    @pl.when(safe_ref[0] == 0)
    def _():
        pens = [causal_pen()] + [pen_ref[i][:1] for i in range(3)]
        pairs = (((bk_ref, bv_ref, 0), (sk_ref, sv_ref, 0)), ((ak_ref, av_ref, 0),) * 2, ((c_ref, c_ref, BLK), (bk_ref, bv_ref, 0)))

        def blocks(g):
            yield kv_ref[:BLK, cut(g)], kv_ref[BLK:, cut(g)]
            for (ek, ev, first), (ok, ov, _) in pairs:
                key = jnp.where(odd, ok[:BLK, cut(g)], ek[:BLK, cut(g)])
                yield key, jnp.where(odd, ov[:BLK, cut(g)], ev[first : first + BLK, cut(g)])

        exact_rows(groups, size, q_ref, blocks, pens, result_ref, out_hbm, sems.at[0])


def routes(n):
    step = n // 4
    ring = [(i, (i + 2) % n) for i in range(n)]
    across = {i: i + 3 for i in range(1, n - 3, 2)}
    first = [n - 3 - step * k for k in (1, 2, 3)] + [2]
    second = [n - 5 - step * k for k in (0, 1, 2)] + [step + 1, 0]
    for at, places in ((n - 3, first), (n - 1, second)):
        for place in places:
            across[at] = place
            at = place - 1
    across.update({i: i + 1 for i in range(0, n, 2) if i not in across})
    swap = [(i, i ^ 1) for i in range(n)]
    return ring, sorted(across.items()), swap


def in_hbm(array):
    return pltpu.with_memory_space_constraint(array, pltpu.HBM)


def after(value, *others):
    return lax.optimization_barrier((value, *others))[0]


def on_device(queries, keys, values_in, docs):
    row_count, width = keys.shape
    groups = width // HD
    size = queries.shape[1] // width
    rows = size * BLK
    n = lax.axis_size("ctx")
    assert row_count == BLK and n % 16 == 0
    ring, across, swap = routes(n)
    cost = pl.CostEstimate(flops=0, bytes_accessed=0, transcendentals=0)
    weights_shape = jax.ShapeDtypeStruct((groups, rows, HD), BF16)
    both_shape = jax.ShapeDtypeStruct((groups, rows, 2 * HD), F32)
    pack_shape = jax.ShapeDtypeStruct((2 * BLK, width), BF16)
    range_shape = jax.ShapeDtypeStruct((2, 8, HD), F32)
    result = jax.ShapeDtypeStruct(queries.shape, BF16)
    dma = pltpu.SemaphoreType.DMA

    def call(kernel, name, out_shape, operands, out_specs=None, in_specs=None, scratch_shapes=(), **options):
        many = isinstance(out_shape, tuple)
        return pl.pallas_call(
            kernel,
            out_shape=out_shape,
            in_specs=in_specs or [VMEM] * len(operands),
            out_specs=out_specs or ((VMEM,) * len(out_shape) if many else VMEM),
            scratch_shapes=scratch_shapes,
            compiler_params=PARAMS,
            cost_estimate=cost,
            name=name,
            **options,
        )(*operands)

    def move(block, route):
        return lax.ppermute(block, "ctx", route)

    def own():
        return call(
            functools.partial(own_kernel, groups, size), "own_block",
            (weights_shape, jax.ShapeDtypeStruct((3, 8, HD), F32), result, pack_shape),
            [in_hbm(x) for x in (docs, queries, keys, values_in)], in_specs=[HBM] * 4,
            scratch_shapes=[pltpu.SMEM(docs.shape, jnp.int32), dma((groups + 3,))],
        )

    def early(*operands):
        return call(
            functools.partial(early_kernel, groups, size), "early_rows",
            (weights_shape, weights_shape, result, result, range_shape), operands,
            out_specs=(VMEM, VMEM, VMEM, HBM, VMEM), scratch_shapes=[dma(())],
        )

    def values(parity, *operands):
        name = ("even", "odd")[parity] + "_values"
        alias = {7: 0} if len(operands) > 7 else {}
        return call(
            functools.partial(values_kernel, groups, size, parity), name, (both_shape, range_shape), operands,
            input_output_aliases=alias,
        )

    def weigh_block(name, distances, *operands):
        return call(
            functools.partial(weights_kernel, groups, size, distances), name, (weights_shape, result), operands,
            in_specs=[VMEM] * 8 + [HBM], out_specs=(VMEM, HBM), input_output_aliases={8: 1},
            scratch_shapes=[pltpu.VMEM(result.shape, BF16), dma(())],
        )

    ak, av = move(keys, ring), move(values_in, ring)
    sk, sv = move(keys, swap), move(values_in, swap)
    w_own, pen, local, block = own()
    block_c = move(after(block, pen), across)
    w_a, w_s, first_rows, stored, early_range = early(local, pen, w_own, block, ak, sk, sv)
    bk = move(after(ak, pen), swap)
    both, so_far = values(1, w_own, w_a, w_s, block, av, sv, early_range)
    bv = move(after(av, both), swap)
    both, so_far = values(0, w_own, w_a, w_s, block, av, sv, so_far, both)
    w_b, stored = weigh_block("third_weights", (1, 3), local, pen, bk, block, sk, sv, early_range, first_rows, in_hbm(stored))
    unit_sems = dma((groups * size // LAST_UNIT,))
    stored, so_far = call(
        functools.partial(complete_kernel, groups, size), "complete_rows", (result, range_shape), (both, w_b, bv, so_far, in_hbm(stored)),
        in_specs=[VMEM] * 4 + [HBM], out_specs=(HBM, VMEM), input_output_aliases={4: 0},
        scratch_shapes=[pltpu.VMEM(result.shape, BF16), unit_sems],
    )
    operands = (local, pen, both, block_c, w_own, w_a, w_b, w_s, block, ak, av, bk, bv, sk, sv, so_far, in_hbm(stored))
    return call(
        functools.partial(last_kernel, groups, size), "last_blocks", result, operands,
        in_specs=[VMEM] * 16 + [HBM], out_specs=HBM, input_output_aliases={16: 0},
        scratch_shapes=[pltpu.VMEM(result.shape, BF16), pltpu.VMEM(range_shape.shape, F32), pltpu.SMEM((1,), jnp.int32), unit_sems],
    )


def solution(mesh):
    return jax.shard_map(
        on_device,
        mesh=mesh,
        in_specs=(
            P(("seq", "ctx"), None),
            P(("seq", "ctx"), None),
            P(("seq", "ctx"), None),
            P("seq"),
        ),
        out_specs=P(("seq", "ctx"), None),
        check_vma=False,
    )
```

```python
import functools
import math

import jax
import jax.numpy as jnp
from jax import lax
from jax.experimental import pallas as pl
from jax.experimental.pallas import tpu as pltpu
from jax.sharding import PartitionSpec as P

HD = 128
BLK = 128
NEG = -1e30
LOW, HIGH = 1e-25, 1e35
EXP2_SCALE = math.log2(math.e) / math.sqrt(HD)
OWN_UNIT, ADD_UNIT, LAST_UNIT = 4, 8, 8
F32 = jnp.float32
BF16 = jnp.bfloat16
VMEM = pl.BlockSpec(memory_space=pltpu.VMEM)
HBM = pl.BlockSpec(memory_space=pltpu.HBM)
PARAMS = pltpu.CompilerParams(vmem_limit_bytes=40 * 1024 * 1024)


def dot_nt(a, b):
    return lax.dot_general(a, b, (((1,), (1,)), ((), ())), preferred_element_type=F32)


def dot_nn(a, b):
    return lax.dot_general(a, b, (((1,), (0,)), ((), ())), preferred_element_type=F32)


def cut(index, width=HD):
    return slice(index * width, (index + 1) * width)


def with_ones(values):
    return jnp.concatenate([values, jnp.ones_like(values)], axis=1)


def unit_queries(q_ref, size, unit):
    g, first, count = unit
    return jnp.concatenate([q_ref[:, cut(g * size + first + h)] for h in range(count)], axis=0)


def unit_rows(unit):
    return slice(unit[1] * BLK, (unit[1] + unit[2]) * BLK)


def units_of(groups, size, count):
    return [(g, first, count) for g in range(groups) for first in range(0, size, count)]


def staggered(units, first, second):
    waiting = None
    for unit in units:
        ready = (unit, first(unit))
        if waiting is not None:
            second(*waiting)
        waiting = ready
    second(*waiting)


def penalty(docs_ref, position, distance):
    source = position - distance
    same = docs_ref[jnp.maximum(source, 0)] == docs_ref[position]
    return jnp.where((source >= 0) & same, 0.0, -NEG).astype(F32)


def weigh(scores, pen):
    return jnp.exp2(scores * EXP2_SCALE - pen).astype(BF16)


def causal_pen():
    row = lax.broadcasted_iota(jnp.int32, (BLK, BLK), 0)
    col = lax.broadcasted_iota(jnp.int32, (BLK, BLK), 1)
    return jnp.where(col <= row, 0.0, -NEG).astype(F32)


def own_kernel(groups, size, docs_hbm, q_hbm, k_hbm, v_hbm, weights_ref, pen_ref, q_ref, kv_ref, docs_ref, sems):
    rest = [
        pltpu.make_async_copy(k_hbm, kv_ref.at[:BLK], sems.at[groups]),
        pltpu.make_async_copy(v_hbm, kv_ref.at[BLK:], sems.at[groups + 1]),
        pltpu.make_async_copy(docs_hbm, docs_ref, sems.at[groups + 2]),
    ]
    copies = []
    for g in range(groups):
        at = cut(g, size * HD)
        copies.append(pltpu.make_async_copy(q_hbm.at[:, at], q_ref.at[:, at], sems.at[g]))
    for copy in rest[:1] + copies + rest[1:]:
        copy.start()
    pen = jnp.concatenate([causal_pen()] * OWN_UNIT, axis=0)
    rest[0].wait()
    for unit in units_of(groups, size, OWN_UNIT):
        g, rows = unit[0], unit_rows(unit)
        if unit[1] == 0:
            copies[g].wait()
        weights_ref[g, rows] = weigh(dot_nt(unit_queries(q_ref, size, unit), kv_ref[:BLK, cut(g)]), pen)
    for copy in rest[1:]:
        copy.wait()
    for i, distance in enumerate((1, 2, 3)):
        pen_ref[i] = jnp.full((8, HD), penalty(docs_ref, lax.axis_index("ctx"), distance), F32)


def weigh_all(groups, size, q_ref, pen, k_ref, weights_ref):
    for unit in units_of(groups, size, ADD_UNIT):
        scores = dot_nt(unit_queries(q_ref, size, unit), k_ref[:BLK, cut(unit[0])])
        weights_ref[unit[0], unit_rows(unit)] = weigh(scores, pen)


def weights_kernel(groups, size, distances, q_ref, pen_ref, k_ref, kv_ref, sk_ref, sv_ref, so_far, rows_ref, _, weights_ref, out_hbm, result_ref, sem):
    position = lax.axis_index("ctx")
    even, odd = (pen_ref[d - 1][:1] for d in distances)

    @pl.when(position > 1)
    def _():
        weigh_all(groups, size, q_ref, jnp.where(lax.rem(position, 2) == 1, odd, even), k_ref, weights_ref)

    @pl.when(position == 1)
    def _():
        copy = pltpu.make_async_copy(rows_ref, out_hbm, sem)
        copy.start()
        copy.wait()

    @pl.when((position <= 1) & jnp.logical_not(is_safe(so_far)))
    def _():
        def blocks(g):
            yield kv_ref[:BLK, cut(g)], kv_ref[BLK:, cut(g)]
            yield sk_ref[:, cut(g)], sv_ref[:, cut(g)]

        exact_rows(groups, size, q_ref, blocks, [causal_pen(), pen_ref[0][:1]], result_ref, out_hbm, sem)


def add_values(unit, weights, values):
    g, rows = unit[0], unit_rows(unit)
    left = jnp.concatenate([w[g, rows] for w in weights], axis=1)
    right = jnp.concatenate([v(g) for v in values], axis=0)
    return dot_nn(left, with_ones(right))


def part(ref, first=0):
    return lambda g: ref[first : first + BLK, cut(g)]


def finish(size, unit, both, result_ref, low_high):
    total = both[:, HD:]
    result = (both[:, :HD] / total).astype(BF16)
    g, first, count = unit
    for h in range(count):
        result_ref[:, cut(g * size + first + h)] = result[cut(h, BLK)]
        if low_high[0] is not None:
            low_high[0] = jnp.minimum(low_high[0], total[cut(h, BLK)])
        low_high[1] = jnp.maximum(low_high[1], total[cut(h, BLK)])


def new_range():
    return [jnp.ones((BLK, HD), F32)] * 2


def note_range(low_high, range_ref):
    if low_high[0] is not None:
        range_ref[0] = jnp.full((8, HD), jnp.min(low_high[0]), F32)
    range_ref[1] = jnp.full((8, HD), jnp.max(low_high[1]), F32)


def is_safe(range_ref):
    in_range = (range_ref[0] > LOW) & (range_ref[1] < HIGH)
    return jnp.min(jnp.where(in_range, 1.0, 0.0)) > 0.5


def exact_rows(groups, size, q_ref, blocks, pens, result_ref, out_hbm, sem):
    for g in range(groups):
        keys, values = zip(*blocks(g))

        def one_head(h, _):
            at = pl.ds(pl.multiple_of((g * size + h) * HD, HD), HD)
            queries = q_ref[:, at]
            scores = [dot_nt(queries, x) - pen for x, pen in zip(keys, pens)]
            top = functools.reduce(jnp.maximum, [jnp.max(x, axis=1, keepdims=True) for x in scores])
            weights = [jnp.exp2((x - top) * EXP2_SCALE) for x in scores]
            total = sum(jnp.sum(w, axis=1, keepdims=True) for w in weights)
            product = sum(dot_nn(w.astype(BF16), x) for w, x in zip(weights, values))
            result_ref[:, at] = (product / total).astype(BF16)
            return 0

        lax.fori_loop(0, size, one_head, 0)
    store = pltpu.make_async_copy(result_ref, out_hbm, sem)
    store.start()
    store.wait()


def early_kernel(
    groups, size, q_ref, pen_ref, own_ref, kv_ref, a_ref, beside_k, wa_ref, weights_ref, out_hbm, range_ref, result_ref, sem,
):
    position = lax.axis_index("ctx")
    range_ref[...] = jnp.ones_like(range_ref)

    @pl.when(position > 1)
    def _():
        weigh_all(groups, size, q_ref, pen_ref[1][:1], a_ref, wa_ref)

    @pl.when(lax.rem(position, 2) == 1)
    def _():
        weigh_all(groups, size, q_ref, pen_ref[0][:1], beside_k, weights_ref)

    def store_all(weights, values):
        low_high = new_range()
        for unit in units_of(groups, size, size):
            finish(size, unit, add_values(unit, weights, values), result_ref, low_high)
        note_range(low_high, range_ref)

    @pl.when(position == 0)
    def _():
        store_all([own_ref], [part(kv_ref, BLK)])
        copy = pltpu.make_async_copy(result_ref, out_hbm, sem)
        copy.start()
        copy.wait()


def values_kernel(groups, size, parity, own_ref, wa_ref, ws_ref, kv_ref, va_ref, vs_ref, so_far, *refs):
    both_ref, range_ref = refs[-2 - parity : len(refs) - parity]
    position = lax.axis_index("ctx")
    range_ref[...] = so_far[...]

    @pl.when((lax.rem(position, 2) == parity) & (position > 1))
    def _():
        weights = [own_ref, wa_ref] + [ws_ref] * parity
        values = [part(kv_ref, BLK), part(va_ref)] + [part(vs_ref)] * parity
        low = jnp.ones((BLK, HD), F32)
        for unit in units_of(groups, size, ADD_UNIT):
            both = add_values(unit, weights, values)
            both_ref[unit[0], unit_rows(unit)] = both
            for h in range(unit[2]):
                low = jnp.minimum(low, both[cut(h, BLK), HD:])
        range_ref[0] = jnp.full((8, HD), jnp.min(low), F32)

    if parity == 1:

        @pl.when(position == 1)
        def _():
            low_high = new_range()
            for unit in units_of(groups, size, ADD_UNIT):
                both = add_values(unit, [own_ref, ws_ref], [part(kv_ref, BLK), part(vs_ref)])
                finish(size, unit, both, refs[-1], low_high)
            note_range(low_high, range_ref)


def out_copies(units, size, result_ref, out_hbm, sems):
    copies = {}
    for n, unit in enumerate(units):
        start = (unit[0] * size + unit[1]) * HD
        at = slice(start, start + unit[2] * HD)
        copies[unit] = pltpu.make_async_copy(result_ref.at[:, at], out_hbm.at[:, at], sems.at[n])
    return copies


def all_here(position):
    return (lax.rem(position, 2) == 1) | (position < 3)


def complete_kernel(groups, size, both_ref, wb_ref, bv_ref, so_far, _, out_hbm, range_ref, result_ref, sems):
    position = lax.axis_index("ctx")
    range_ref[...] = so_far[...]

    @pl.when(all_here(position) & (position > 1))
    def _():
        units = units_of(groups, size, LAST_UNIT)
        copies = out_copies(units, size, result_ref, out_hbm, sems)
        low_high = [None, new_range()[1]]
        for unit in units:
            both = both_ref[unit[0], unit_rows(unit)] + add_values(unit, [wb_ref], [part(bv_ref)])
            finish(size, unit, both, result_ref, low_high)
            copies[unit].start()
        note_range(low_high, range_ref)
        for copy in copies.values():
            copy.wait()


def last_kernel(
    groups, size, q_ref, pen_ref, both_ref, c_ref, own_ref, wa_ref, wb_ref, ws_ref, kv_ref,
    ak_ref, av_ref, bk_ref, bv_ref, sk_ref, sv_ref, so_far, _, out_hbm, result_ref, range_ref, safe_ref, sems,
):
    position = lax.axis_index("ctx")
    odd = lax.rem(position, 2) == 1
    units = units_of(groups, size, LAST_UNIT)
    copies = out_copies(units, size, result_ref, out_hbm, sems)
    range_ref[...] = so_far[...]
    waits = jnp.logical_not(all_here(position))
    safe_ref[0] = 1

    def check():
        safe_ref[0] = jnp.where(is_safe(range_ref), 1, 0)

    @pl.when(jnp.logical_not(waits) & (position > 1))
    def _():
        check()

    @pl.when(waits)
    def _():
        low_high = [None, new_range()[1]]
        pen = pen_ref[2][:1]

        def first(unit):
            return weigh(dot_nt(unit_queries(q_ref, size, unit), c_ref[:BLK, cut(unit[0])]), pen)

        def second(unit, weights):
            g, at = unit[0], unit_rows(unit)
            weights = jnp.concatenate([wb_ref[g, at], weights], axis=1)
            values = jnp.concatenate([bv_ref[:, cut(g)], c_ref[BLK:, cut(g)]], axis=0)
            both = both_ref[g, at] + dot_nn(weights, with_ones(values))
            finish(size, unit, both, result_ref, low_high)
            copies[unit].start()

        staggered(units, first, second)
        note_range(low_high, range_ref)
        check()
        for copy in copies.values():
            copy.wait()

    @pl.when(safe_ref[0] == 0)
    def _():
        pens = [causal_pen()] + [pen_ref[i][:1] for i in range(3)]
        pairs = (((bk_ref, bv_ref, 0), (sk_ref, sv_ref, 0)), ((ak_ref, av_ref, 0),) * 2, ((c_ref, c_ref, BLK), (bk_ref, bv_ref, 0)))

        def blocks(g):
            yield kv_ref[:BLK, cut(g)], kv_ref[BLK:, cut(g)]
            for (ek, ev, first), (ok, ov, _) in pairs:
                key = jnp.where(odd, ok[:BLK, cut(g)], ek[:BLK, cut(g)])
                yield key, jnp.where(odd, ov[:BLK, cut(g)], ev[first : first + BLK, cut(g)])

        exact_rows(groups, size, q_ref, blocks, pens, result_ref, out_hbm, sems.at[0])


def routes(n):
    step = n // 4
    ring = [(i, (i + 2) % n) for i in range(n)]
    across = {i: i + 3 for i in range(1, n - 3, 2)}
    first = [n - 3 - step * k for k in (1, 2, 3)] + [2]
    second = [n - 5 - step * k for k in (0, 1, 2)] + [step + 1, 0]
    for at, places in ((n - 3, first), (n - 1, second)):
        for place in places:
            across[at] = place
            at = place - 1
    across.update({i: i + 1 for i in range(0, n, 2) if i not in across})
    swap = [(i, i ^ 1) for i in range(n)]
    return ring, sorted(across.items()), swap


def in_hbm(array):
    return pltpu.with_memory_space_constraint(array, pltpu.HBM)


def after(value, *others):
    return lax.optimization_barrier((value, *others))[0]


def on_device(queries, keys, values_in, docs):
    row_count, width = keys.shape
    groups = width // HD
    size = queries.shape[1] // width
    rows = size * BLK
    n = lax.axis_size("ctx")
    assert row_count == BLK and n % 16 == 0
    ring, across, swap = routes(n)
    cost = pl.CostEstimate(flops=0, bytes_accessed=0, transcendentals=0)
    weights_shape = jax.ShapeDtypeStruct((groups, rows, HD), BF16)
    both_shape = jax.ShapeDtypeStruct((groups, rows, 2 * HD), F32)
    pack_shape = jax.ShapeDtypeStruct((2 * BLK, width), BF16)
    range_shape = jax.ShapeDtypeStruct((2, 8, HD), F32)
    result = jax.ShapeDtypeStruct(queries.shape, BF16)
    dma = pltpu.SemaphoreType.DMA

    def call(kernel, name, out_shape, operands, out_specs=None, in_specs=None, scratch_shapes=(), **options):
        many = isinstance(out_shape, tuple)
        return pl.pallas_call(
            kernel,
            out_shape=out_shape,
            in_specs=in_specs or [VMEM] * len(operands),
            out_specs=out_specs or ((VMEM,) * len(out_shape) if many else VMEM),
            scratch_shapes=scratch_shapes,
            compiler_params=PARAMS,
            cost_estimate=cost,
            name=name,
            **options,
        )(*operands)

    def move(block, route):
        return lax.ppermute(block, "ctx", route)

    def own():
        return call(
            functools.partial(own_kernel, groups, size), "own_block",
            (weights_shape, jax.ShapeDtypeStruct((3, 8, HD), F32), result, pack_shape),
            [in_hbm(x) for x in (docs, queries, keys, values_in)], in_specs=[HBM] * 4,
            scratch_shapes=[pltpu.SMEM(docs.shape, jnp.int32), dma((groups + 3,))],
        )

    def early(*operands):
        return call(
            functools.partial(early_kernel, groups, size), "early_rows",
            (weights_shape, weights_shape, result, range_shape), operands,
            out_specs=(VMEM, VMEM, HBM, VMEM), scratch_shapes=[pltpu.VMEM(result.shape, BF16), dma(())],
        )

    def values(parity, *operands):
        name = ("even", "odd")[parity] + "_values"
        alias = {7: 0} if len(operands) > 7 else {}
        return call(
            functools.partial(values_kernel, groups, size, parity), name,
            (both_shape, range_shape) + (result,) * parity, operands,
            input_output_aliases=alias,
        )

    def weigh_block(name, distances, *operands):
        return call(
            functools.partial(weights_kernel, groups, size, distances), name, (weights_shape, result), operands,
            in_specs=[VMEM] * 8 + [HBM], out_specs=(VMEM, HBM), input_output_aliases={8: 1},
            scratch_shapes=[pltpu.VMEM(result.shape, BF16), dma(())],
        )

    ak, av = move(keys, ring), move(values_in, ring)
    sk, sv = move(keys, swap), move(values_in, swap)
    w_own, pen, local, block = own()
    block_c = move(after(block, pen), across)
    w_a, w_s, stored, early_range = early(local, pen, w_own, block, ak, sk)
    bk = move(after(ak, pen), swap)
    both, so_far, first_rows = values(1, w_own, w_a, w_s, block, av, sv, early_range)
    first_range = so_far
    bv = move(after(av, both), swap)
    both, so_far = values(0, w_own, w_a, w_s, block, av, sv, so_far, both)
    w_b, stored = weigh_block("third_weights", (1, 3), local, pen, bk, block, sk, sv, first_range, first_rows, in_hbm(stored))
    unit_sems = dma((groups * size // LAST_UNIT,))
    stored, so_far = call(
        functools.partial(complete_kernel, groups, size), "complete_rows", (result, range_shape), (both, w_b, bv, so_far, in_hbm(stored)),
        in_specs=[VMEM] * 4 + [HBM], out_specs=(HBM, VMEM), input_output_aliases={4: 0},
        scratch_shapes=[pltpu.VMEM(result.shape, BF16), unit_sems],
    )
    operands = (local, pen, both, block_c, w_own, w_a, w_b, w_s, block, ak, av, bk, bv, sk, sv, so_far, in_hbm(stored))
    return call(
        functools.partial(last_kernel, groups, size), "last_blocks", result, operands,
        in_specs=[VMEM] * 16 + [HBM], out_specs=HBM, input_output_aliases={16: 0},
        scratch_shapes=[pltpu.VMEM(result.shape, BF16), pltpu.VMEM(range_shape.shape, F32), pltpu.SMEM((1,), jnp.int32), unit_sems],
    )


def solution(mesh):
    return jax.shard_map(
        on_device,
        mesh=mesh,
        in_specs=(
            P(("seq", "ctx"), None),
            P(("seq", "ctx"), None),
            P(("seq", "ctx"), None),
            P("seq"),
        ),
        out_specs=P(("seq", "ctx"), None),
        check_vma=False,
    )
```
